128 devices in a mesh: row: 8 (over z, y_lo), col: 16 (over x, y_hi, core).
Axes of the slice: x: 4, y: 4 (y_hi: 2, y_lo: 2; y = y_hi * 2 + y_lo), z: 4, core: 2. Of those that a mesh axis runs over, the one named last changes fastest.
Arguments:
- picture: float32 [3, 512, 2048], P(None, 'row', 'col'), may hold values from -6 to 6
- membrane: float32 [64, 256, 1024], P('row', 'col'), may hold values from -3 to 3
- dictionary: bfloat16 [1024, 3072], replicated, may hold values from -4 to 4
- momentum: float32 [1024, 3072], P(('row', 'col')), may hold values from -5 to 5
Outputs:
- final_codes: float32 [64, 256, 1024], P('row', 'col')
- new_dictionary: float32 [1024, 3072], P(('row', 'col'))
- new_momentum: float32 [1024, 3072], P(('row', 'col'))
The draws below stay inside these ranges and needn't reach their ends.
All inputs are finite; a program needn't handle non-finite values.
Results may differ from the reference program's by a relative error of at most 0.0032.
Values may be sent and summed in bfloat16 or wider, within the bound.
A program may use at most 64 MiB of HBM per device.

```python
import jax
import jax.numpy as jnp
from jax import lax

K = 1024
CHANNELS = 3
PATCH_SIDE = 32
STRIDE = 8
SWEEPS = 2
PATCH = 3072
SROWS = 64
SCOLS = 256
HEIGHT = 512
WIDTH = 2048


def block_levels(rng, extent, split, least, largest):
    loudness = 1.0
    for axis_at, parts in split:
        steps = jax.random.uniform(jax.random.fold_in(jax.random.fold_in(rng, 6), axis_at), (parts,), jnp.float32, least / len(split), largest / len(split))
        loudness = loudness * jnp.repeat(jnp.exp(steps), extent[axis_at] // parts).reshape((-1,) + (1,) * (len(extent) - 1 - axis_at))
    return loudness


def scatter_about(rng, shape, deviation, bound, shards=(), kind=jnp.bfloat16):
    loudness = block_levels(rng, shape, shards, -0.22, 0.18) if shards else 1.0
    drawn = jax.random.normal(rng, shape, jnp.float32) * deviation * loudness
    return jnp.minimum(jnp.maximum(drawn, -bound), bound).astype(kind)


def setup_inputs(seed: int = 0) -> dict:
    key_of = jax.random.split(jax.random.key(seed), 5)
    return {
        "picture": scatter_about(key_of[0], (CHANNELS, HEIGHT, WIDTH), 1.0, 6.0, ((1, 8), (2, 16)), jnp.float32),
        "membrane": scatter_about(key_of[1], (SROWS, SCOLS, K), 0.5, 3.0, ((0, 8), (1, 16)), jnp.float32),
        "dictionary": scatter_about(key_of[2], (K, PATCH), 1.0, 4.0),
        "momentum": scatter_about(key_of[3], (K, PATCH), 1.0, 5.0, ((0, 128),), jnp.float32),
    }


THRESHOLD = 0.25
RELAXATION = 0.1
DECAY = 0.9
LEARNING = 0.25
EPSILON = 1e-05

def shrink(potential):
    return potential - jnp.clip(potential, -THRESHOLD, THRESHOLD)

def cells_of(picture):
    channels, height, width_px = picture.shape
    blocked = picture.reshape(channels, height // STRIDE, STRIDE, width_px // STRIDE, STRIDE)
    return blocked.transpose(1, 3, 0, 2, 4).reshape(height // STRIDE, width_px // STRIDE, channels * STRIDE * STRIDE)

def reconstruct(coding, dictionary):
    site_rows, site_cols, atom_count = coding.shape
    span_cells = PATCH_SIDE // STRIDE
    cell_size = CHANNELS * STRIDE * STRIDE
    atom_scale = PATCH ** (-0.5)
    flat_codes = coding.reshape(site_rows * site_cols, atom_count)
    canvas = jnp.zeros((site_rows + span_cells - 1, site_cols + span_cells - 1, cell_size), jnp.float32)
    for row_off in range(span_cells):
        for col_off in range(span_cells):
            first_col = (row_off * span_cells + col_off) * cell_size
            placed = jnp.dot(flat_codes, dictionary[:, first_col:first_col + cell_size], preferred_element_type=jnp.float32) * atom_scale
            canvas = canvas.at[row_off:row_off + site_rows, col_off:col_off + site_cols].add(placed.reshape(site_rows, site_cols, cell_size))
    return canvas[:site_rows, :site_cols]

def windows(residual):
    site_rows, site_cols, cell_size = residual.shape
    span_cells = PATCH_SIDE // STRIDE
    padded = jnp.pad(residual, ((0, span_cells - 1), (0, span_cells - 1), (0, 0)))
    return [padded[row_off:row_off + site_rows, col_off:col_off + site_cols].reshape(site_rows * site_cols, cell_size) for row_off in range(span_cells) for col_off in range(span_cells)]

def reference(picture, membrane, dictionary, momentum):
    pixels = cells_of(picture)
    site_rows, site_cols, atom_count = membrane.shape
    cell_size = CHANNELS * STRIDE * STRIDE
    atom_scale = PATCH ** (-0.5)
    potential = membrane
    for repeat in range(SWEEPS):
        active = shrink(potential)
        coding = active.astype(jnp.bfloat16)
        residual = (pixels - reconstruct(coding, dictionary)).astype(jnp.bfloat16)
        drive_term = jnp.zeros((site_rows * site_cols, atom_count), jnp.float32)
        for index_block, window in enumerate(windows(residual)):
            first_col = index_block * cell_size
            drive_term = drive_term + lax.dot_general(window, dictionary[:, first_col:first_col + cell_size], (((1,), (1,)), ((), ())), preferred_element_type=jnp.float32)
        drive_term = drive_term * atom_scale
        potential = potential + RELAXATION * (drive_term.reshape(site_rows, site_cols, atom_count) + active - potential)
    final_codes = shrink(potential)
    coding = final_codes.astype(jnp.bfloat16)
    residual = (pixels - reconstruct(coding, dictionary)).astype(jnp.bfloat16)
    flat_codes = coding.reshape(site_rows * site_cols, atom_count)
    pieces = [lax.dot_general(flat_codes, window, (((0,), (0,)), ((), ())), preferred_element_type=jnp.float32) * atom_scale for window in windows(residual)]
    learning = jnp.concatenate(pieces, axis=1)
    new_momentum = DECAY * momentum + learning
    weights = dictionary.astype(jnp.float32) + LEARNING * new_momentum
    new_dictionary = weights * lax.rsqrt(lax.optimization_barrier(jnp.mean(weights * weights, axis=1, keepdims=True)) + EPSILON)
    return (final_codes, new_dictionary, new_momentum)
```

```python
import jax
import jax.numpy as jnp
from jax import lax
from jax.sharding import PartitionSpec as P

PATCH_SIDE = 32
STRIDE = 8
SWEEPS = 2


THRESHOLD = 0.25
RELAXATION = 0.1
DECAY = 0.9
LEARNING = 0.25
EPSILON = 1e-05


def passed_along(block, axis, distance):
    devices = range(lax.axis_size(axis))
    route = [(i - distance, i) for i in devices if i - distance in devices]
    return lax.ppermute(block, axis, route)


def shrink(potential):
    return potential - jnp.clip(potential, -THRESHOLD, THRESHOLD)


def cells_of(picture):
    channels, height, width_px = picture.shape
    blocked = picture.reshape(channels, height // STRIDE, STRIDE, width_px // STRIDE, STRIDE)
    return blocked.transpose(1, 3, 0, 2, 4).reshape(
        height // STRIDE, width_px // STRIDE, channels * STRIDE * STRIDE
    )


def place_atoms(coding, dictionary):
    site_rows, site_cols, atom_count = coding.shape
    span_cells = PATCH_SIDE // STRIDE
    cell_size = dictionary.shape[1] // (span_cells * span_cells)
    atom_scale = dictionary.shape[1] ** (-0.5)
    placed = (
        jnp.dot(
            coding.reshape(site_rows * site_cols, atom_count),
            dictionary,
            preferred_element_type=jnp.float32,
        )
        * atom_scale
    )
    placed = placed.reshape(site_rows, site_cols, span_cells, span_cells, cell_size)
    canvas = None
    for row_off in range(span_cells):
        for col_off in range(span_cells):
            shifted = jnp.pad(
                placed[:, :, row_off, col_off],
                ((row_off, span_cells - 1 - row_off), (col_off, span_cells - 1 - col_off), (0, 0)),
            )
            canvas = shifted if canvas is None else canvas + shifted
    return canvas


def reconstruct(coding, dictionary):
    site_rows, site_cols = (coding.shape[0], coding.shape[1])
    margin = PATCH_SIDE // STRIDE - 1
    canvas = place_atoms(coding, dictionary)
    lower_spill = passed_along(canvas[site_rows:], "row", 1)
    canvas = jnp.concatenate([canvas[:margin] + lower_spill, canvas[margin:site_rows]], axis=0)
    beside = passed_along(canvas[:, site_cols:], "col", 1)
    return jnp.concatenate([canvas[:, :margin] + beside, canvas[:, margin:site_cols]], axis=1)


def extend(residual):
    margin = PATCH_SIDE // STRIDE - 1
    below_rim = passed_along(residual[:margin], "row", -1)
    tall_part = jnp.concatenate([residual, below_rim], axis=0)
    beside = passed_along(tall_part[:, :margin], "col", -1)
    return jnp.concatenate([tall_part, beside], axis=1)


def patches_of(wide_part, site_rows, site_cols):
    span_cells = PATCH_SIDE // STRIDE
    blocks = [
        wide_part[row_off : row_off + site_rows, col_off : col_off + site_cols]
        for row_off in range(span_cells)
        for col_off in range(span_cells)
    ]
    return jnp.stack(blocks, axis=2).reshape(site_rows * site_cols, -1)


def shards(picture, membrane, dictionary, momentum):
    pixels = cells_of(picture)
    site_rows, site_cols, atom_count = membrane.shape
    patch_len = dictionary.shape[1]
    atom_scale = patch_len ** (-0.5)
    potential = membrane
    for repeat in range(SWEEPS):
        active = shrink(potential)
        coding = active.astype(jnp.bfloat16)
        residual = (pixels - reconstruct(coding, dictionary)).astype(jnp.bfloat16)
        patches = patches_of(extend(residual), site_rows, site_cols)
        drive_term = (
            lax.dot_general(
                patches, dictionary, (((1,), (1,)), ((), ())), preferred_element_type=jnp.float32
            )
            * atom_scale
        )
        potential = potential + RELAXATION * (
            drive_term.reshape(site_rows, site_cols, atom_count) + active - potential
        )
    final_codes = shrink(potential)
    coding = final_codes.astype(jnp.bfloat16)
    residual = (pixels - reconstruct(coding, dictionary)).astype(jnp.bfloat16)
    margin = PATCH_SIDE // STRIDE - 1
    rows = lax.axis_size("row")
    beside = passed_along(residual[:, :margin], "col", -1)
    strip = lax.all_gather(
        jnp.concatenate([residual, beside], axis=1), "row", axis=0, tiled=True
    )
    strip = jnp.pad(strip, ((0, margin), (0, 0), (0, 0)))
    final_patches = patches_of(strip, rows * site_rows, site_cols)
    strip_codes = lax.all_to_all(
        coding.reshape(site_rows * site_cols, rows, atom_count // rows),
        "row",
        split_axis=1,
        concat_axis=0,
        tiled=True,
    ).reshape(rows * site_rows * site_cols, atom_count // rows)
    owned_rows = momentum.shape[0]
    learning = lax.psum_scatter(
        lax.dot_general(
            strip_codes, final_patches, (((0,), (0,)), ((), ())), preferred_element_type=jnp.float32
        )
        * atom_scale,
        "col",
        scatter_dimension=0,
        tiled=True,
    )
    owner_index = lax.axis_index(("row", "col"))
    own_atoms = lax.dynamic_slice_in_dim(
        dictionary, owner_index * owned_rows, owned_rows, 0
    ).astype(jnp.float32)
    new_momentum = DECAY * momentum + learning
    weights = own_atoms + LEARNING * new_momentum
    new_dictionary = weights * lax.rsqrt(
        jnp.mean(weights * weights, axis=1, keepdims=True) + EPSILON
    )
    return (final_codes, new_dictionary, new_momentum)


def solution(mesh):
    return jax.shard_map(
        shards,
        mesh=mesh,
        in_specs=(P(None, "row", "col"), P("row", "col", None), P(), P(("row", "col"), None)),
        out_specs=(P("row", "col", None), P(("row", "col"), None), P(("row", "col"), None)),
        check_vma=False,
    )
```

```python
import functools

import jax
import jax.numpy as jnp
from jax import lax
from jax.experimental import pallas as pl
from jax.experimental.pallas import tpu as pltpu
from jax.sharding import PartitionSpec as P

STRIDE = 8
SPAN = 4
MARGIN = SPAN - 1
SWEEPS = 2

THRESHOLD = 0.25
RELAXATION = 0.1
DECAY = 0.9
LEARNING = 0.25
EPSILON = 1e-05

F32 = jnp.float32
BF16 = jnp.bfloat16
MESH = pl.DeviceIdType.MESH


def shrink(potential):
    return potential - jnp.clip(potential, -THRESHOLD, THRESHOLD)


def cells_of(picture):
    channels, height, width_px = picture.shape
    blocked = picture.reshape(channels, height // STRIDE, STRIDE, width_px // STRIDE, STRIDE)
    return blocked.transpose(1, 3, 0, 2, 4).reshape(
        height // STRIDE, width_px // STRIDE, channels * STRIDE * STRIDE
    )


def peers_of(rows, cols):
    offsets = {(j, 0) for j in range(rows)} | {(0, j) for j in range(cols)}
    offsets |= {(j, k % cols) for j in range(rows) for k in (1, -1)}
    return sorted(offsets - {(0, 0)})


def kernel(
    rows, cols,
    pixels_ref, membrane_ref, dictionary_hbm, momentum_ref,
    codes_out, dictionary_out, momentum_out,
    dic, pot, coding, acc, zbuf, cbuf, ext, wide,
    down_out, side_out, down_in, side_in, diag_in,
    res_ref, edge_ref, up_in, left_in, corner_in,
    codes_t, strip_codes, strip_res, strip_edge, share_out, share_in,
    load_sem, spill_send, spill_recv, halo_send, halo_recv,
    code_send, code_recv, res_send, res_recv, rim_send, rim_recv,
    share_send, share_recv,
):
    site_rows, site_cols, cell = pixels_ref.shape
    sites, atoms = pot.shape
    patch = dic.shape[1]
    band = patch // SPAN
    pair = band // 2
    scale = patch ** (-0.5)
    share = atoms // rows
    owned = momentum_ref.shape[0]
    half = patch // 2
    me_r, me_c = lax.axis_index("row"), lax.axis_index("col")

    def at(dr, dc):
        return (lax.rem(me_r + dr % rows, rows), lax.rem(me_c + dc % cols, cols))

    def remote(src, dst, send, recv, dr, dc):
        return pltpu.make_async_remote_copy(
            src_ref=src, dst_ref=dst, send_sem=send, recv_sem=recv,
            device_id=at(dr, dc), device_id_type=MESH,
        )

    loads = [
        pltpu.make_async_copy(
            dictionary_hbm.at[:, pl.ds(d * band, band)],
            dic.at[:, pl.ds(d * band, band)],
            load_sem.at[d],
        )
        for d in range(SPAN)
    ]
    for load in loads:
        load.start()

    barrier = pltpu.get_barrier_semaphore()
    peers = peers_of(rows, cols)
    for dr, dc in peers:
        pl.semaphore_signal(barrier, inc=1, device_id=at(dr, dc), device_id_type=MESH)

    pot[...] = membrane_ref[...]
    coding[...] = shrink(membrane_ref[...]).astype(BF16)
    wide[rows * site_rows :] = jnp.zeros((MARGIN, site_cols, band), BF16)
    zbuf[...] = jnp.zeros_like(zbuf)
    cbuf[...] = jnp.zeros_like(cbuf)
    pl.semaphore_wait(barrier, len(peers))

    sub = lax.broadcasted_iota(jnp.int32, (1, 8, cell), 1)
    low = sub < 4

    def packed(tall):
        n = tall.shape[0] // 2
        split = tall.reshape(n, 2, 8, cell)
        return split[:, 0] + pltpu.roll(split[:, 1], 4, 1)

    def unpacked(tight):
        n = tight.shape[0]
        both = jnp.stack([tight, pltpu.roll(tight, 4, 1)], axis=1)
        return jnp.where(low, both.reshape(2 * n, 8, cell), 0.0)

    def reconstruct(phase):
        for d in range(SPAN):
            if phase == 0:
                loads[d].wait()
            placed = jnp.dot(
                coding[...], dic[:, d * band : (d + 1) * band], preferred_element_type=F32
            ).reshape(site_rows, site_cols, band)
            if d == 0:
                acc[0:site_rows] = placed
            else:
                acc[d : d + site_rows - 1] += placed[: site_rows - 1]
                acc[d + site_rows - 1] = placed[site_rows - 1]
        zbuf[:, 0:site_cols] = acc[:, :, :pair]
        zbuf[:, site_cols:] = jnp.zeros((site_rows + MARGIN, 8, pair), F32)
        zbuf[:, 2 : site_cols + 2] += acc[:, :, pair:]
        every = zbuf[...]
        cbuf[: site_rows + MARGIN] = every[:, :, :cell]
        cbuf[: site_rows + MARGIN, 1 : site_cols + 3] += every[:, : site_cols + 2, cell:]
        down_out[phase] = cbuf[site_rows : site_rows + MARGIN, :site_cols] * scale
        side_out[phase] = packed(cbuf[:, site_cols:] * scale)
        n = site_rows // 2
        copies = [
            remote(side_out.at[phase, pl.ds(0, n)], side_in.at[phase],
                   spill_send.at[phase, 0], spill_recv.at[phase, 0], 0, 1),
            remote(down_out.at[phase], down_in.at[phase],
                   spill_send.at[phase, 1], spill_recv.at[phase, 1], 1, 0),
            remote(side_out.at[phase, pl.ds(n, 2)], diag_in.at[phase],
                   spill_send.at[phase, 2], spill_recv.at[phase, 2], 1, 1),
        ]
        for copy in copies:
            copy.start()
        own = pixels_ref[...] - cbuf[:site_rows, :site_cols] * scale
        for copy in copies:
            copy.wait()
        from_above = jnp.where(me_r > 0, down_in[phase], 0.0)
        from_left = jnp.where(me_c > 0, unpacked(side_in[phase]), 0.0)
        from_both = jnp.where(
            jnp.logical_and(me_r > 0, me_c > 0), unpacked(diag_in[phase]), 0.0
        )
        cbuf[:site_rows, :site_cols] = own
        cbuf[:MARGIN, :site_cols] -= from_above
        cbuf[:site_rows, :8] -= from_left
        cbuf[:SPAN, :8] -= from_both
        residual = cbuf[:site_rows, :site_cols].astype(BF16)
        res_ref[phase] = residual
        left_cols = jnp.where(low, residual.astype(F32)[:, :8], 0.0)
        edge_ref[phase] = packed(left_cols).reshape(site_rows * 4, cell).astype(BF16)

    def widen(n):
        x = ext[:n]
        return jnp.concatenate(
            [x[:, k : k + site_cols] for k in range(SPAN)], axis=2
        ).astype(BF16)

    for sweep in range(SWEEPS):
        reconstruct(sweep)
        copies = [
            remote(edge_ref.at[sweep], left_in.at[sweep],
                   halo_send.at[sweep, 0], halo_recv.at[sweep, 0], 0, -1),
            remote(res_ref.at[sweep, pl.ds(0, MARGIN)], up_in.at[sweep],
                   halo_send.at[sweep, 1], halo_recv.at[sweep, 1], -1, 0),
            remote(edge_ref.at[sweep, pl.ds(0, 16)], corner_in.at[sweep],
                   halo_send.at[sweep, 2], halo_recv.at[sweep, 2], -1, -1),
        ]
        for copy in copies:
            copy.start()
        ext[:site_rows, :site_cols] = res_ref[sweep].astype(F32)
        for copy in copies:
            copy.wait()
        inside_r, inside_c = me_r < rows - 1, me_c < cols - 1
        ext[site_rows : site_rows + MARGIN, :site_cols] = jnp.where(
            inside_r, up_in[sweep].astype(F32), 0.0
        )
        beside = unpacked(left_in[sweep].astype(F32).reshape(site_rows // 2, 8, cell))
        ext[:site_rows, site_cols:] = jnp.where(inside_c, beside, 0.0)
        below = unpacked(corner_in[sweep].astype(F32).reshape(2, 8, cell))
        ext[site_rows:, site_cols:] = jnp.where(
            jnp.logical_and(inside_r, inside_c), below[:MARGIN], 0.0
        )
        wide[: site_rows + MARGIN] = widen(site_rows + MARGIN)
        last = sweep == SWEEPS - 1
        step = 256 if atoms % 256 == 0 else 128
        for first in range(0, atoms, step):
            drive = jnp.zeros((sites, step), F32)
            for d in range(SPAN):
                drive += lax.dot_general(
                    wide[d : d + site_rows].reshape(sites, band),
                    dic[first : first + step, d * band : (d + 1) * band],
                    (((1,), (1,)), ((), ())),
                    preferred_element_type=F32,
                )
            old = pot[:, first : first + step]
            new = old + RELAXATION * (drive * scale + shrink(old) - old)
            codes = shrink(new)
            coding[:, first : first + step] = codes.astype(BF16)
            if last:
                codes_out[:, first : first + step] = codes
                codes_t[first : first + step] = codes.T.astype(BF16)
            else:
                pot[:, first : first + step] = new

    def share_of(row):
        return codes_t.at[pl.ds(pl.multiple_of(row * share, share), share)]

    def place_of(row):
        return strip_codes.at[:, pl.ds(pl.multiple_of(row * sites, sites), sites)]

    code_copies = [
        remote(share_of(at(j, 0)[0]), place_of(me_r), code_send.at[j], code_recv.at[j], j, 0)
        for j in range(1, rows)
    ]
    for copy in code_copies:
        copy.start()
    place_of(me_r)[...] = share_of(me_r)[...]

    reconstruct(SWEEPS)
    rim_copies = [
        remote(edge_ref.at[SWEEPS], strip_edge.at[j], rim_send.at[j], rim_recv.at[j], j, -1)
        for j in range(rows)
    ]
    res_copies = [None] + [
        remote(res_ref.at[SWEEPS], strip_res.at[j], res_send.at[j], res_recv.at[j], j, 0)
        for j in range(1, rows)
    ]
    for j in range(rows):
        rim_copies[j].start()
        if j:
            res_copies[j].start()
    for j in range(rows):
        rim_copies[j].wait()
        if j:
            res_copies[j].wait()
        block = strip_res[j] if j else res_ref[SWEEPS]
        ext[:site_rows, :site_cols] = block.astype(F32)
        beside = unpacked(strip_edge[j].astype(F32).reshape(site_rows // 2, 8, cell))
        ext[:site_rows, site_cols:] = jnp.where(me_c < cols - 1, beside, 0.0)
        source = at(-j, 0)[0]
        wide[pl.ds(source * site_rows, site_rows)] = widen(site_rows)
    for copy in code_copies:
        copy.wait()

    tall = rows * site_rows
    for e in range(2):
        parts = [
            jnp.dot(
                strip_codes[...],
                wide[d : d + tall].reshape(tall * site_cols, band),
                preferred_element_type=F32,
            ).reshape(cols, owned, band)
            for d in (e, e + 2)
        ]
        share_out[:, :, e * band : (e + 1) * band] = jnp.concatenate(parts, axis=1).astype(BF16)
    share_copies = [
        remote(share_out.at[at(0, j)[1]], share_in.at[j], share_send.at[j], share_recv.at[j], 0, j)
        for j in range(1, cols)
    ]
    for copy in share_copies:
        copy.start()
    total = share_out[me_c].astype(F32)
    for j in range(1, cols):
        share_copies[j - 1].wait()
        total += share_in[j].astype(F32)

    for h in range(2):
        momentum_out[:, h * half : (h + 1) * half] = (
            DECAY * momentum_ref[:, h * half : (h + 1) * half]
            + total[h * owned : (h + 1) * owned] * scale
        )
    tile = 2 * owned
    index = me_r * cols + me_c
    first = pl.multiple_of(lax.div(index, 2) * tile, tile)
    both = dic[pl.ds(first, tile)].astype(F32)
    own_atoms = jnp.where(lax.rem(index, 2) == 1, both[owned:], both[:owned])
    weights = own_atoms + LEARNING * momentum_out[...]
    dictionary_out[...] = weights * lax.rsqrt(
        jnp.mean(weights * weights, axis=1, keepdims=True) + EPSILON
    )


def shards(picture, membrane, dictionary, momentum):
    pixels = cells_of(picture)
    site_rows, site_cols, atoms = membrane.shape
    sites = site_rows * site_cols
    patch = dictionary.shape[1]
    cell = pixels.shape[2]
    band, half = patch // SPAN, patch // 2
    owned = momentum.shape[0]
    rows, cols = lax.axis_size("row"), lax.axis_size("col")
    phases = SWEEPS + 1
    vmem, dma = pltpu.VMEM, pltpu.SemaphoreType.DMA
    in_vmem = pl.BlockSpec(memory_space=pltpu.VMEM)
    codes, new_dictionary, new_momentum = pl.pallas_call(
        functools.partial(kernel, rows, cols),
        out_shape=(
            jax.ShapeDtypeStruct((sites, atoms), F32),
            jax.ShapeDtypeStruct((owned, patch), F32),
            jax.ShapeDtypeStruct((owned, patch), F32),
        ),
        in_specs=[in_vmem, in_vmem, pl.BlockSpec(memory_space=pl.ANY), in_vmem],
        out_specs=(in_vmem, in_vmem, in_vmem),
        scratch_shapes=[
            vmem((atoms, patch), BF16),
            vmem((sites, atoms), F32),
            vmem((sites, atoms), BF16),
            vmem((site_rows + MARGIN, site_cols, band), F32),
            vmem((site_rows + MARGIN, site_cols + 8, band // 2), F32),
            vmem((site_rows + SPAN, site_cols + 8, cell), F32),
            vmem((site_rows + MARGIN, site_cols + 8, cell), F32),
            vmem((rows * site_rows + MARGIN, site_cols, band), BF16),
            vmem((phases, MARGIN, site_cols, cell), F32),
            vmem((phases, site_rows // 2 + 2, 8, cell), F32),
            vmem((phases, MARGIN, site_cols, cell), F32),
            vmem((phases, site_rows // 2, 8, cell), F32),
            vmem((phases, 2, 8, cell), F32),
            vmem((phases, site_rows, site_cols, cell), BF16),
            vmem((phases, site_rows * 4, cell), BF16),
            vmem((SWEEPS, MARGIN, site_cols, cell), BF16),
            vmem((SWEEPS, site_rows * 4, cell), BF16),
            vmem((SWEEPS, 16, cell), BF16),
            vmem((atoms, sites), BF16),
            vmem((atoms // rows, rows * sites), BF16),
            vmem((rows, site_rows, site_cols, cell), BF16),
            vmem((rows, site_rows * 4, cell), BF16),
            vmem((cols, 2 * owned, half), BF16),
            vmem((cols, 2 * owned, half), BF16),
            dma((SPAN,)),
            dma((phases, 3)), dma((phases, 3)),
            dma((SWEEPS, 3)), dma((SWEEPS, 3)),
            dma((rows,)), dma((rows,)),
            dma((rows,)), dma((rows,)),
            dma((rows,)), dma((rows,)),
            dma((cols,)), dma((cols,)),
        ],
        compiler_params=pltpu.CompilerParams(
            collective_id=0, has_side_effects=True, vmem_limit_bytes=48 * 2**20
        ),
    )(pixels, membrane.reshape(sites, atoms), dictionary, momentum)
    return codes.reshape(membrane.shape), new_dictionary, new_momentum


def solution(mesh):
    return jax.shard_map(
        shards,
        mesh=mesh,
        in_specs=(P(None, "row", "col"), P("row", "col", None), P(), P(("row", "col"), None)),
        out_specs=(P("row", "col", None), P(("row", "col"), None), P(("row", "col"), None)),
        check_vma=False,
    )
```

```python
import functools

import jax
import jax.numpy as jnp
from jax import lax
from jax.experimental import pallas as pl
from jax.experimental.pallas import tpu as pltpu
from jax.sharding import PartitionSpec as P

STRIDE = 8
SPAN = 4
MARGIN = SPAN - 1
SWEEPS = 2

THRESHOLD = 0.25
RELAXATION = 0.1
DECAY = 0.9
LEARNING = 0.25
EPSILON = 1e-05

F32 = jnp.float32
BF16 = jnp.bfloat16
MESH = pl.DeviceIdType.MESH


def shrink(potential):
    return potential - jnp.clip(potential, -THRESHOLD, THRESHOLD)


def cells_of(picture):
    channels, height, width_px = picture.shape
    blocked = picture.reshape(channels, height // STRIDE, STRIDE, width_px // STRIDE, STRIDE)
    return blocked.transpose(1, 3, 0, 2, 4).reshape(
        height // STRIDE, width_px // STRIDE, channels * STRIDE * STRIDE
    )


def peers_of(rows, cols):
    offsets = {(j, 0) for j in range(rows)} | {(0, j) for j in range(cols)}
    offsets |= {(j, k % cols) for j in range(rows) for k in (1, -1)}
    return sorted(offsets - {(0, 0)})


def kernel(
    rows, cols,
    pixels_ref, membrane_hbm, dictionary_hbm, momentum_hbm,
    codes_out, dictionary_out, momentum_out,
    dic, pot, coding, acc, zbuf, cbuf, ext, wide,
    down_out, up_out, t_out, l_out, above_in, below_in, left_in, right_in, corner_in,
    res_ref, edge_ref,
    codes_t, strip_codes, strip_res, strip_edge, share_out, share_in,
    momentum_ref, load_sem, spill_send, spill_recv,
    code_send, code_recv, res_send, res_recv, rim_send, rim_recv,
    share_send, share_recv,
):
    site_rows, site_cols, cell = pixels_ref.shape
    sites, atoms = pot.shape
    patch = dic.shape[1]
    band = patch // SPAN
    pair = band // 2
    scale = patch ** (-0.5)
    share = atoms // rows
    owned = momentum_ref.shape[0]
    half = patch // 2
    me_r, me_c = lax.axis_index("row"), lax.axis_index("col")

    def at(dr, dc):
        return (lax.rem(me_r + dr % rows, rows), lax.rem(me_c + dc % cols, cols))

    def remote(src, dst, send, recv, dr, dc):
        return pltpu.make_async_remote_copy(
            src_ref=src, dst_ref=dst, send_sem=send, recv_sem=recv,
            device_id=at(dr, dc), device_id_type=MESH,
        )

    loads = [
        pltpu.make_async_copy(
            dictionary_hbm.at[:, pl.ds(d * band, band)],
            dic.at[:, pl.ds(d * band, band)],
            load_sem.at[d],
        )
        for d in range(SPAN)
    ]
    membrane_load = pltpu.make_async_copy(membrane_hbm, pot, load_sem.at[SPAN])
    momentum_load = pltpu.make_async_copy(momentum_hbm, momentum_ref, load_sem.at[SPAN + 1])
    for load in [membrane_load] + loads + [momentum_load]:
        load.start()

    barrier = pltpu.get_barrier_semaphore()
    peers = peers_of(rows, cols)
    for dr, dc in peers:
        pl.semaphore_signal(barrier, inc=1, device_id=at(dr, dc), device_id_type=MESH)

    wide[rows * site_rows :] = jnp.zeros((MARGIN, site_cols, band), BF16)
    zbuf[...] = jnp.zeros_like(zbuf)
    cbuf[...] = jnp.zeros_like(cbuf)
    membrane_load.wait()
    coding[...] = shrink(pot[...]).astype(BF16)
    sent = []

    def send(copies):
        for copy in copies:
            copy.start()
        sent.extend(copies)

    sub = lax.broadcasted_iota(jnp.int32, (1, 8, cell), 1)
    low = sub < 4

    def packed(tall):
        n = tall.shape[0] // 2
        split = tall.reshape(n, 2, 8, cell)
        return split[:, 0] + pltpu.roll(split[:, 1], 4, 1)

    def unpacked(tight):
        n = tight.shape[0]
        both = jnp.stack([tight, pltpu.roll(tight, 4, 1)], axis=1)
        return jnp.where(low, both.reshape(2 * n, 8, cell), 0.0)

    def reconstruct(phase):
        for d in range(SPAN):
            if phase == 0:
                loads[d].wait()
            placed = jnp.dot(
                coding[...], dic[:, d * band : (d + 1) * band], preferred_element_type=F32
            ).reshape(site_rows, site_cols, band)
            if d == 0:
                acc[0:site_rows] = placed
            else:
                acc[d : d + site_rows - 1] += placed[: site_rows - 1]
                acc[d + site_rows - 1] = placed[site_rows - 1]
        zbuf[:, 0:site_cols] = acc[:, :, :pair]
        zbuf[:, site_cols:] = jnp.zeros((site_rows + MARGIN, 8, pair), F32)
        zbuf[:, 2 : site_cols + 2] += acc[:, :, pair:]
        every = zbuf[...]
        cbuf[: site_rows + MARGIN] = every[:, :, :cell]
        cbuf[: site_rows + MARGIN, 1 : site_cols + 3] += every[:, : site_cols + 2, cell:]
        ext[...] = cbuf[...] * -scale
        ext[:site_rows, :site_cols] += pixels_ref[...]
        beyond = packed(ext[:, site_cols:])
        within = packed(jnp.where(low, ext[:, :8], 0.0))
        tight = lambda part: part.reshape(-1, cell)
        tail, head = slice(site_rows // 2, None), slice(0, 2)
        last = phase == SWEEPS
        t_out[phase] = tight(beyond).astype(BF16)
        down_out[phase] = jnp.concatenate(
            [tight(ext[site_rows : site_rows + MARGIN, :site_cols]), tight(beyond[tail])]
        ).astype(BF16)
        if not last:
            l_out[phase] = tight(within).astype(BF16)
            up_out[phase] = jnp.concatenate(
                [tight(ext[:MARGIN, :site_cols]), tight(beyond[head])]
            ).astype(BF16)
        own_t = site_rows * 4
        main = MARGIN * site_cols
        corner = pl.ds(own_t, 16)

        def hop(k, src, dst, dr, dc):
            return remote(src, dst, spill_send.at[phase, k], spill_recv.at[phase, k], dr, dc)

        if last:
            copies = [
                hop(0, t_out.at[phase, corner], corner_in.at[phase, 0], 1, 1),
                hop(1, down_out.at[phase, pl.ds(0, main)], above_in.at[phase, pl.ds(0, main)], 1, 0),
                hop(2, t_out.at[phase, pl.ds(0, own_t)], left_in.at[phase, pl.ds(0, own_t)], 0, 1),
            ]
        else:
            copies = [
                hop(0, t_out.at[phase, corner], corner_in.at[phase, 0], 1, 1),
                hop(3, l_out.at[phase, pl.ds(0, 16)], corner_in.at[phase, 1], -1, -1),
                hop(4, l_out.at[phase, corner], corner_in.at[phase, 2], 1, -1),
                hop(5, t_out.at[phase, pl.ds(0, 16)], corner_in.at[phase, 3], -1, 1),
                hop(1, down_out.at[phase], above_in.at[phase], 1, 0),
                hop(6, up_out.at[phase], below_in.at[phase], -1, 0),
                hop(2, t_out.at[phase], left_in.at[phase], 0, 1),
                hop(7, l_out.at[phase], right_in.at[phase], 0, -1),
            ]
        if phase == 0:
            pl.semaphore_wait(barrier, len(peers))
        send(copies)
        return copies

    has_above, has_below = me_r > 0, me_r < rows - 1
    has_left, has_right = me_c > 0, me_c < cols - 1

    def loose(ref_part):
        return unpacked(ref_part.astype(F32).reshape(-1, 8, cell))

    def gather_spill(phase, copies):
        last = phase == SWEEPS
        for copy in copies:
            copy.wait_recv()
        main = MARGIN * site_cols
        own_t = site_rows * 4
        own, far_r, far_c = slice(0, site_rows), slice(site_rows, None), slice(site_cols, None)
        ext[:MARGIN, :site_cols] += jnp.where(
            has_above, above_in[phase, :main].astype(F32).reshape(MARGIN, site_cols, cell), 0.0
        )
        reach = own_t if last else own_t + 16
        ext[: reach // 4, :8] += jnp.where(has_left, loose(left_in[phase, :reach]), 0.0)
        ext[:SPAN, :8] += jnp.where(
            jnp.logical_and(has_above, has_left), loose(corner_in[phase, 0]), 0.0
        )
        if last:
            return
        ext[far_r, :8] += jnp.where(has_left, loose(corner_in[phase, 3]), 0.0)
        side = ext[:, far_c] + loose(right_in[phase])
        side_head = side[:SPAN] + jnp.where(
            has_above, loose(above_in[phase, main:]) + loose(corner_in[phase, 2]), 0.0
        )
        side_tail = side[site_rows:] + loose(below_in[phase, main:]) + loose(corner_in[phase, 1])
        ext[:, far_c] = jnp.where(has_right, side, 0.0)
        ext[:SPAN, far_c] = jnp.where(has_right, side_head, 0.0)
        ext[far_r, far_c] = jnp.where(jnp.logical_and(has_right, has_below), side_tail, 0.0)
        under = ext[site_rows : site_rows + MARGIN, :site_cols] + below_in[phase, :main].astype(
            F32
        ).reshape(MARGIN, site_cols, cell)
        ext[site_rows : site_rows + MARGIN, :site_cols] = jnp.where(has_below, under, 0.0)

    def widen(n):
        x = ext[:n]
        return jnp.concatenate(
            [x[:, k : k + site_cols] for k in range(SPAN)], axis=2
        ).astype(BF16)

    for sweep in range(SWEEPS):
        gather_spill(sweep, reconstruct(sweep))
        wide[: site_rows + MARGIN] = widen(site_rows + MARGIN)
        last = sweep == SWEEPS - 1
        step = 256 if atoms % 256 == 0 else 128
        for first in range(0, atoms, step):
            drive = jnp.zeros((sites, step), F32)
            for d in range(SPAN):
                drive += lax.dot_general(
                    wide[d : d + site_rows].reshape(sites, band),
                    dic[first : first + step, d * band : (d + 1) * band],
                    (((1,), (1,)), ((), ())),
                    preferred_element_type=F32,
                )
            old = pot[:, first : first + step]
            new = old + RELAXATION * (drive * scale + shrink(old) - old)
            codes = shrink(new)
            coding[:, first : first + step] = codes.astype(BF16)
            if last:
                codes_out[:, first : first + step] = codes
                codes_t[first : first + step] = codes.T.astype(BF16)
            else:
                pot[:, first : first + step] = new

    def share_of(row):
        return codes_t.at[pl.ds(pl.multiple_of(row * share, share), share)]

    def place_of(row):
        return strip_codes.at[:, pl.ds(pl.multiple_of(row * sites, sites), sites)]

    code_copies = [
        remote(share_of(at(j, 0)[0]), place_of(me_r), code_send.at[j], code_recv.at[j], j, 0)
        for j in range(1, rows)
    ]
    send(code_copies)
    place_of(me_r)[...] = share_of(me_r)[...]

    gather_spill(SWEEPS, reconstruct(SWEEPS))
    residual = ext[:site_rows, :site_cols].astype(BF16)
    res_ref[...] = residual
    left_cols = jnp.where(low, residual.astype(F32)[:, :8], 0.0)
    edge_ref[...] = packed(left_cols).reshape(site_rows * 4, cell).astype(BF16)
    rim_copies = [
        remote(edge_ref, strip_edge.at[j], rim_send.at[j], rim_recv.at[j], j, -1)
        for j in range(rows)
    ]
    res_copies = [None] + [
        remote(res_ref, strip_res.at[j], res_send.at[j], res_recv.at[j], j, 0)
        for j in range(1, rows)
    ]
    for j in range(rows):
        send([rim_copies[j]] + ([res_copies[j]] if j else []))
    for j in range(rows):
        rim_copies[j].wait_recv()
        if j:
            res_copies[j].wait_recv()
        block = strip_res[j] if j else res_ref[...]
        ext[:site_rows, :site_cols] = block.astype(F32)
        ext[:site_rows, site_cols:] = jnp.where(has_right, loose(strip_edge[j]), 0.0)
        source = at(-j, 0)[0]
        wide[pl.ds(source * site_rows, site_rows)] = widen(site_rows)
    for copy in code_copies:
        copy.wait_recv()

    tall = rows * site_rows
    for e in range(2):
        parts = [
            jnp.dot(
                strip_codes[...],
                wide[d : d + tall].reshape(tall * site_cols, band),
                preferred_element_type=F32,
            ).reshape(cols, owned, band)
            for d in (e, e + 2)
        ]
        share_out[:, :, e * band : (e + 1) * band] = jnp.concatenate(parts, axis=1).astype(BF16)
    share_copies = [
        remote(share_out.at[at(0, j)[1]], share_in.at[j], share_send.at[j], share_recv.at[j], 0, j)
        for j in range(1, cols)
    ]
    send(share_copies)
    total = share_out[me_c].astype(F32)
    for j in range(1, cols):
        share_copies[j - 1].wait_recv()
        total += share_in[j].astype(F32)

    momentum_load.wait()
    for h in range(2):
        momentum_out[:, h * half : (h + 1) * half] = (
            DECAY * momentum_ref[:, h * half : (h + 1) * half]
            + total[h * owned : (h + 1) * owned] * scale
        )
    tile = 2 * owned
    index = me_r * cols + me_c
    first = pl.multiple_of(lax.div(index, 2) * tile, tile)
    both = dic[pl.ds(first, tile)].astype(F32)
    own_atoms = jnp.where(lax.rem(index, 2) == 1, both[owned:], both[:owned])
    weights = own_atoms + LEARNING * momentum_out[...]
    dictionary_out[...] = weights * lax.rsqrt(
        jnp.mean(weights * weights, axis=1, keepdims=True) + EPSILON
    )
    for copy in sent:
        copy.wait_send()


def shards(picture, membrane, dictionary, momentum):
    pixels = cells_of(picture)
    site_rows, site_cols, atoms = membrane.shape
    sites = site_rows * site_cols
    patch = dictionary.shape[1]
    cell = pixels.shape[2]
    band, half = patch // SPAN, patch // 2
    owned = momentum.shape[0]
    rows, cols = lax.axis_size("row"), lax.axis_size("col")
    phases = SWEEPS + 1
    vmem, dma = pltpu.VMEM, pltpu.SemaphoreType.DMA
    anywhere = pl.BlockSpec(memory_space=pltpu.HBM)
    in_vmem = pl.BlockSpec(memory_space=pltpu.VMEM)
    codes, new_dictionary, new_momentum = pl.pallas_call(
        functools.partial(kernel, rows, cols),
        out_shape=(
            jax.ShapeDtypeStruct((sites, atoms), F32),
            jax.ShapeDtypeStruct((owned, patch), F32),
            jax.ShapeDtypeStruct((owned, patch), F32),
        ),
        in_specs=[in_vmem, anywhere, anywhere, anywhere],
        out_specs=(in_vmem, in_vmem, in_vmem),
        scratch_shapes=[
            vmem((atoms, patch), BF16),
            vmem((sites, atoms), F32),
            vmem((sites, atoms), BF16),
            vmem((site_rows + MARGIN, site_cols, band), F32),
            vmem((site_rows + MARGIN, site_cols + 8, band // 2), F32),
            vmem((site_rows + SPAN, site_cols + 8, cell), F32),
            vmem((site_rows + SPAN, site_cols + 8, cell), F32),
            vmem((rows * site_rows + MARGIN, site_cols, band), BF16),
            vmem((phases, MARGIN * site_cols + 16, cell), BF16),
            vmem((phases, MARGIN * site_cols + 16, cell), BF16),
            vmem((phases, (site_rows + SPAN) * 4, cell), BF16),
            vmem((phases, (site_rows + SPAN) * 4, cell), BF16),
            vmem((phases, MARGIN * site_cols + 16, cell), BF16),
            vmem((phases, MARGIN * site_cols + 16, cell), BF16),
            vmem((phases, (site_rows + SPAN) * 4, cell), BF16),
            vmem((phases, (site_rows + SPAN) * 4, cell), BF16),
            vmem((phases, 4, 16, cell), BF16),
            vmem((site_rows, site_cols, cell), BF16),
            vmem((site_rows * 4, cell), BF16),
            vmem((atoms, sites), BF16),
            vmem((atoms // rows, rows * sites), BF16),
            vmem((rows, site_rows, site_cols, cell), BF16),
            vmem((rows, site_rows * 4, cell), BF16),
            vmem((cols, 2 * owned, half), BF16),
            vmem((cols, 2 * owned, half), BF16),
            vmem((owned, patch), F32),
            dma((SPAN + 2,)),
            dma((phases, 8)), dma((phases, 8)),
            dma((rows,)), dma((rows,)),
            dma((rows,)), dma((rows,)),
            dma((rows,)), dma((rows,)),
            dma((cols,)), dma((cols,)),
        ],
        compiler_params=pltpu.CompilerParams(
            collective_id=0, has_side_effects=True, vmem_limit_bytes=48 * 2**20
        ),
    )(pixels, membrane.reshape(sites, atoms), dictionary, momentum)
    return codes.reshape(membrane.shape), new_dictionary, new_momentum


def solution(mesh):
    return jax.shard_map(
        shards,
        mesh=mesh,
        in_specs=(P(None, "row", "col"), P("row", "col", None), P(), P(("row", "col"), None)),
        out_specs=(P("row", "col", None), P(("row", "col"), None), P(("row", "col"), None)),
        check_vma=False,
    )
```

```python
import functools

import jax
import jax.numpy as jnp
from jax import lax
from jax.experimental import pallas as pl
from jax.experimental.pallas import tpu as pltpu
from jax.sharding import PartitionSpec as P

STRIDE = 8
SPAN = 4
MARGIN = SPAN - 1
SWEEPS = 2

THRESHOLD = 0.25
RELAXATION = 0.1
DECAY = 0.9
LEARNING = 0.25
EPSILON = 1e-05

F32 = jnp.float32
BF16 = jnp.bfloat16
MESH = pl.DeviceIdType.MESH


def shrink(potential):
    return potential - jnp.clip(potential, -THRESHOLD, THRESHOLD)


def cells_of(picture):
    channels = picture.shape[0]
    x = picture.reshape(-1, STRIDE, 128)
    y_at = lax.broadcasted_iota(jnp.int32, (1, STRIDE, 128), 1)
    lane = lax.broadcasted_iota(jnp.int32, (1, STRIDE, 128), 2)
    for bit in (1, 2, 4):
        from_later = pltpu.roll(pltpu.roll(x, STRIDE - bit, 1), STRIDE * bit, 2)
        from_earlier = pltpu.roll(pltpu.roll(x, bit, 1), 128 - STRIDE * bit, 2)
        y_bit = (y_at & bit) != 0
        g_bit = (lane & (STRIDE * bit)) != 0
        x = jnp.where(y_bit == g_bit, x, jnp.where(g_bit, from_later, from_earlier))
    x = x.reshape(channels, -1, STRIDE, 128)
    turned = pltpu.roll(x.reshape(-1, STRIDE, 128), 64, 2).reshape(x.shape)
    lower = lane < 64
    left = jnp.concatenate(
        [jnp.where(lower, x[0], turned[1]), jnp.where(lower, turned[0], x[1])], axis=1
    )
    right = jnp.concatenate([x[2], turned[2]], axis=1)
    return jnp.concatenate([left, right[:, :, :64]], axis=2)


def tightened(x):
    n = x.shape[0] // 2
    ends = jnp.concatenate([x[:n, :, 128:], x[n:, :, 128:]], axis=2)
    return jnp.concatenate([x[:, :, :128], ends], axis=0)


def untightened(t):
    n = t.shape[0] * 2 // 3
    ends = jnp.concatenate([t[n:, :, :64], t[n:, :, 64:]], axis=0)
    return jnp.concatenate([t[:n], ends], axis=2)


def peers_of(rows, cols):
    offsets = {(j, 0) for j in range(rows)} | {(0, j) for j in range(cols)}
    offsets |= {(j, k % cols) for j in range(rows) for k in (1, -1)}
    return sorted(offsets - {(0, 0)})


def kernel(
    rows, cols,
    picture_ref, membrane_hbm, dictionary_hbm, momentum_hbm,
    codes_out, dictionary_out, momentum_out,
    dic, dic_t, pot, coding, cells_ref, acc, zbuf, cbuf, ext, wide,
    down_out, up_out, t_out, l_out, above_in, below_in, left_in, right_in, corner_in,
    res_ref, edge_ref,
    codes_t, strip_codes, strip_res, strip_edge, share_out, share_in,
    momentum_ref, load_sem, spill_send, spill_recv,
    code_send, code_recv, res_send, res_recv, rim_send, rim_recv,
    share_send, share_recv,
):
    site_rows, site_cols, cell = cells_ref.shape
    sites, atoms = pot.shape
    patch = dic.shape[1]
    band = patch // SPAN
    pair = band // 2
    scale = patch ** (-0.5)
    share = atoms // rows
    owned = momentum_ref.shape[0]
    half = patch // 2
    me_r, me_c = lax.axis_index("row"), lax.axis_index("col")

    def at(dr, dc):
        return (lax.rem(me_r + dr % rows, rows), lax.rem(me_c + dc % cols, cols))

    def remote(src, dst, send, recv, dr, dc):
        return pltpu.make_async_remote_copy(
            src_ref=src, dst_ref=dst, send_sem=send, recv_sem=recv,
            device_id=at(dr, dc), device_id_type=MESH,
        )

    loads = [
        pltpu.make_async_copy(
            dictionary_hbm.at[:, pl.ds(d * band, band)],
            dic.at[:, pl.ds(d * band, band)],
            load_sem.at[d],
        )
        for d in range(SPAN)
    ]
    membrane_load = pltpu.make_async_copy(membrane_hbm, pot, load_sem.at[SPAN])
    momentum_load = pltpu.make_async_copy(momentum_hbm, momentum_ref, load_sem.at[SPAN + 1])
    for load in [membrane_load] + loads + [momentum_load]:
        load.start()

    barrier = pltpu.get_barrier_semaphore()
    peers = peers_of(rows, cols)
    for dr, dc in peers:
        pl.semaphore_signal(barrier, inc=1, device_id=at(dr, dc), device_id_type=MESH)

    wide[rows * site_rows :] = jnp.zeros((MARGIN, site_cols, band), BF16)
    zbuf[...] = jnp.zeros_like(zbuf)
    cbuf[...] = jnp.zeros_like(cbuf)
    cells_ref[...] = cells_of(picture_ref[...])
    membrane_load.wait()
    coding[...] = shrink(pot[...]).astype(BF16)
    sent = []

    def send(copies):
        for copy in copies:
            copy.start()
        sent.extend(copies)

    sub = lax.broadcasted_iota(jnp.int32, (1, 8, cell), 1)
    low = sub < 4

    def packed(tall):
        n = tall.shape[0] // 2
        split = tall.reshape(n, 2, 8, cell)
        return split[:, 0] + pltpu.roll(split[:, 1], 4, 1)

    def unpacked(tight):
        n = tight.shape[0]
        both = jnp.stack([tight, pltpu.roll(tight, 4, 1)], axis=1)
        return jnp.where(low, both.reshape(2 * n, 8, cell), 0.0)

    def reconstruct(phase):
        for d in range(SPAN):
            if phase == 0:
                loads[d].wait()
            placed = jnp.dot(
                coding[...], dic[:, d * band : (d + 1) * band], preferred_element_type=F32
            ).reshape(site_rows, site_cols, band)
            if d == 0:
                acc[0:site_rows] = placed
            else:
                acc[d : d + site_rows - 1] += placed[: site_rows - 1]
                acc[d + site_rows - 1] = placed[site_rows - 1]
        zbuf[:, 0:site_cols] = acc[:, :, :pair]
        zbuf[:, site_cols:] = jnp.zeros((site_rows + MARGIN, 8, pair), F32)
        zbuf[:, 2 : site_cols + 2] += acc[:, :, pair:]
        every = zbuf[...]
        cbuf[: site_rows + MARGIN] = every[:, :, :cell]
        cbuf[: site_rows + MARGIN, 1 : site_cols + 3] += every[:, : site_cols + 2, cell:]
        ext[...] = cbuf[...] * -scale
        ext[:site_rows, :site_cols] += cells_ref[...]
        beyond = packed(ext[:, site_cols:])
        within = packed(jnp.where(low, ext[:, :8], 0.0))
        tight = lambda part: part.reshape(-1, cell)
        tail, head = slice(site_rows // 2, None), slice(0, 2)
        last = phase == SWEEPS
        t_out[phase] = tight(beyond).astype(BF16)
        down_out[phase] = jnp.concatenate(
            [tight(ext[site_rows : site_rows + MARGIN, :site_cols]), tight(beyond[tail])]
        ).astype(BF16)
        if not last:
            l_out[phase] = tight(within).astype(BF16)
            up_out[phase] = jnp.concatenate(
                [tight(ext[:MARGIN, :site_cols]), tight(beyond[head])]
            ).astype(BF16)
        own_t = site_rows * 4
        main = MARGIN * site_cols
        corner = pl.ds(own_t, 16)

        def hop(k, src, dst, dr, dc):
            return remote(src, dst, spill_send.at[phase, k], spill_recv.at[phase, k], dr, dc)

        if last:
            copies = [
                hop(0, t_out.at[phase, corner], corner_in.at[phase, 0], 1, 1),
                hop(1, down_out.at[phase, pl.ds(0, main)], above_in.at[phase, pl.ds(0, main)], 1, 0),
                hop(2, t_out.at[phase, pl.ds(0, own_t)], left_in.at[phase, pl.ds(0, own_t)], 0, 1),
            ]
        else:
            copies = [
                hop(0, t_out.at[phase, corner], corner_in.at[phase, 0], 1, 1),
                hop(3, l_out.at[phase, pl.ds(0, 16)], corner_in.at[phase, 1], -1, -1),
                hop(4, l_out.at[phase, corner], corner_in.at[phase, 2], 1, -1),
                hop(5, t_out.at[phase, pl.ds(0, 16)], corner_in.at[phase, 3], -1, 1),
                hop(1, down_out.at[phase], above_in.at[phase], 1, 0),
                hop(6, up_out.at[phase], below_in.at[phase], -1, 0),
                hop(2, t_out.at[phase], left_in.at[phase], 0, 1),
                hop(7, l_out.at[phase], right_in.at[phase], 0, -1),
            ]
        if phase == 0:
            pl.semaphore_wait(barrier, len(peers))
        send(copies)
        if phase == 0:
            for first in range(0, atoms, 256):
                for d in range(SPAN):
                    dic_t[d * band : (d + 1) * band, first : first + 256] = dic[
                        first : first + 256, d * band : (d + 1) * band
                    ].T
        return copies

    has_above, has_below = me_r > 0, me_r < rows - 1
    has_left, has_right = me_c > 0, me_c < cols - 1

    def loose(ref_part):
        return unpacked(ref_part.astype(F32).reshape(-1, 8, cell))

    def gather_spill(phase, copies):
        last = phase == SWEEPS
        for copy in copies:
            copy.wait_recv()
        main = MARGIN * site_cols
        own_t = site_rows * 4
        own, far_r, far_c = slice(0, site_rows), slice(site_rows, None), slice(site_cols, None)
        ext[:MARGIN, :site_cols] += jnp.where(
            has_above, above_in[phase, :main].astype(F32).reshape(MARGIN, site_cols, cell), 0.0
        )
        reach = own_t if last else own_t + 16
        ext[: reach // 4, :8] += jnp.where(has_left, loose(left_in[phase, :reach]), 0.0)
        ext[:SPAN, :8] += jnp.where(
            jnp.logical_and(has_above, has_left), loose(corner_in[phase, 0]), 0.0
        )
        if last:
            return
        ext[far_r, :8] += jnp.where(has_left, loose(corner_in[phase, 3]), 0.0)
        side = ext[:, far_c] + loose(right_in[phase])
        side_head = side[:SPAN] + jnp.where(
            has_above, loose(above_in[phase, main:]) + loose(corner_in[phase, 2]), 0.0
        )
        side_tail = side[site_rows:] + loose(below_in[phase, main:]) + loose(corner_in[phase, 1])
        ext[:, far_c] = jnp.where(has_right, side, 0.0)
        ext[:SPAN, far_c] = jnp.where(has_right, side_head, 0.0)
        ext[far_r, far_c] = jnp.where(jnp.logical_and(has_right, has_below), side_tail, 0.0)
        under = ext[site_rows : site_rows + MARGIN, :site_cols] + below_in[phase, :main].astype(
            F32
        ).reshape(MARGIN, site_cols, cell)
        ext[site_rows : site_rows + MARGIN, :site_cols] = jnp.where(has_below, under, 0.0)

    def widen(n):
        x = ext[:n]
        return jnp.concatenate(
            [x[:, k : k + site_cols] for k in range(SPAN)], axis=2
        ).astype(BF16)

    for sweep in range(SWEEPS):
        gather_spill(sweep, reconstruct(sweep))
        wide[: site_rows + MARGIN] = widen(site_rows + MARGIN)
        last = sweep == SWEEPS - 1
        step = 256 if atoms % 256 == 0 else 128
        for first in range(0, atoms, step):
            drive = jnp.zeros((sites, step), F32)
            for d in range(SPAN):
                drive += jnp.dot(
                    wide[d : d + site_rows].reshape(sites, band),
                    dic_t[d * band : (d + 1) * band, first : first + step],
                    preferred_element_type=F32,
                )
            old = pot[:, first : first + step]
            new = old + RELAXATION * (drive * scale + shrink(old) - old)
            codes = shrink(new)
            coding[:, first : first + step] = codes.astype(BF16)
            if last:
                codes_out[:, first : first + step] = codes
                codes_t[first : first + step] = codes.T.astype(BF16)
            else:
                pot[:, first : first + step] = new

    def share_of(row):
        return codes_t.at[pl.ds(pl.multiple_of(row * share, share), share)]

    def place_of(row):
        return strip_codes.at[:, pl.ds(pl.multiple_of(row * sites, sites), sites)]

    code_copies = [
        remote(share_of(at(j, 0)[0]), place_of(me_r), code_send.at[j], code_recv.at[j], j, 0)
        for j in range(1, rows)
    ]
    send(code_copies)
    place_of(me_r)[...] = share_of(me_r)[...]

    gather_spill(SWEEPS, reconstruct(SWEEPS))
    residual = ext[:site_rows, :site_cols].astype(BF16).astype(F32)
    res_ref[...] = tightened(residual).astype(BF16)
    left_cols = packed(jnp.where(low, residual[:, :8], 0.0))
    edge_ref[...] = tightened(left_cols).reshape(-1, 128).astype(BF16)
    rim_copies = [
        remote(edge_ref, strip_edge.at[j], rim_send.at[j], rim_recv.at[j], j, -1)
        for j in range(rows)
    ]
    res_copies = [None] + [
        remote(res_ref, strip_res.at[j], res_send.at[j], res_recv.at[j], j, 0)
        for j in range(1, rows)
    ]
    for j in range(rows):
        send([rim_copies[j]] + ([res_copies[j]] if j else []))
    for j in range(rows):
        rim_copies[j].wait_recv()
        if j:
            res_copies[j].wait_recv()
        block = strip_res[j] if j else res_ref[...]
        ext[:site_rows, :site_cols] = untightened(block.astype(F32))
        ext[:site_rows, site_cols:] = jnp.where(has_right, unpacked(untightened(strip_edge[j].astype(F32).reshape(-1, 8, 128))), 0.0)
        source = at(-j, 0)[0]
        wide[pl.ds(source * site_rows, site_rows)] = widen(site_rows)
    for copy in code_copies:
        copy.wait_recv()

    tall = rows * site_rows
    for e in range(2):
        parts = [
            jnp.dot(
                strip_codes[...],
                wide[d : d + tall].reshape(tall * site_cols, band),
                preferred_element_type=F32,
            ).reshape(cols, owned, band)
            for d in (e, e + 2)
        ]
        share_out[:, :, e * band : (e + 1) * band] = jnp.concatenate(parts, axis=1).astype(BF16)
    share_copies = [
        remote(share_out.at[at(0, j)[1]], share_in.at[j], share_send.at[j], share_recv.at[j], 0, j)
        for j in range(1, cols)
    ]
    send(share_copies)
    total = share_out[me_c].astype(F32)
    for j in range(1, cols):
        share_copies[j - 1].wait_recv()
        total += share_in[j].astype(F32)

    momentum_load.wait()
    for h in range(2):
        momentum_out[:, h * half : (h + 1) * half] = (
            DECAY * momentum_ref[:, h * half : (h + 1) * half]
            + total[h * owned : (h + 1) * owned] * scale
        )
    tile = 2 * owned
    index = me_r * cols + me_c
    first = pl.multiple_of(lax.div(index, 2) * tile, tile)
    both = dic[pl.ds(first, tile)].astype(F32)
    own_atoms = jnp.where(lax.rem(index, 2) == 1, both[owned:], both[:owned])
    weights = own_atoms + LEARNING * momentum_out[...]
    dictionary_out[...] = weights * lax.rsqrt(
        jnp.mean(weights * weights, axis=1, keepdims=True) + EPSILON
    )
    for copy in sent:
        copy.wait_send()


def shards(picture, membrane, dictionary, momentum):
    site_rows, site_cols, atoms = membrane.shape
    sites = site_rows * site_cols
    patch = dictionary.shape[1]
    cell = patch // SPAN // SPAN
    band, half = patch // SPAN, patch // 2
    owned = momentum.shape[0]
    rows, cols = lax.axis_size("row"), lax.axis_size("col")
    phases = SWEEPS + 1
    vmem, dma = pltpu.VMEM, pltpu.SemaphoreType.DMA
    anywhere = pl.BlockSpec(memory_space=pltpu.HBM)
    in_vmem = pl.BlockSpec(memory_space=pltpu.VMEM)
    codes, new_dictionary, new_momentum = pl.pallas_call(
        functools.partial(kernel, rows, cols),
        out_shape=(
            jax.ShapeDtypeStruct((sites, atoms), F32),
            jax.ShapeDtypeStruct((owned, patch), F32),
            jax.ShapeDtypeStruct((owned, patch), F32),
        ),
        in_specs=[in_vmem, anywhere, anywhere, anywhere],
        out_specs=(in_vmem, in_vmem, in_vmem),
        scratch_shapes=[
            vmem((atoms, patch), BF16),
            vmem((patch, atoms), BF16),
            vmem((sites, atoms), F32),
            vmem((sites, atoms), BF16),
            vmem((site_rows, site_cols, cell), F32),
            vmem((site_rows + MARGIN, site_cols, band), F32),
            vmem((site_rows + MARGIN, site_cols + 8, band // 2), F32),
            vmem((site_rows + SPAN, site_cols + 8, cell), F32),
            vmem((site_rows + SPAN, site_cols + 8, cell), F32),
            vmem((rows * site_rows + MARGIN, site_cols, band), BF16),
            vmem((phases, MARGIN * site_cols + 16, cell), BF16),
            vmem((phases, MARGIN * site_cols + 16, cell), BF16),
            vmem((phases, (site_rows + SPAN) * 4, cell), BF16),
            vmem((phases, (site_rows + SPAN) * 4, cell), BF16),
            vmem((phases, MARGIN * site_cols + 16, cell), BF16),
            vmem((phases, MARGIN * site_cols + 16, cell), BF16),
            vmem((phases, (site_rows + SPAN) * 4, cell), BF16),
            vmem((phases, (site_rows + SPAN) * 4, cell), BF16),
            vmem((phases, 4, 16, cell), BF16),
            vmem((site_rows * 3 // 2, site_cols, 128), BF16),
            vmem((site_rows * 6, 128), BF16),
            vmem((atoms, sites), BF16),
            vmem((atoms // rows, rows * sites), BF16),
            vmem((rows, site_rows * 3 // 2, site_cols, 128), BF16),
            vmem((rows, site_rows * 6, 128), BF16),
            vmem((cols, 2 * owned, half), BF16),
            vmem((cols, 2 * owned, half), BF16),
            vmem((owned, patch), F32),
            dma((SPAN + 2,)),
            dma((phases, 8)), dma((phases, 8)),
            dma((rows,)), dma((rows,)),
            dma((rows,)), dma((rows,)),
            dma((rows,)), dma((rows,)),
            dma((cols,)), dma((cols,)),
        ],
        compiler_params=pltpu.CompilerParams(
            collective_id=0, has_side_effects=True, vmem_limit_bytes=48 * 2**20
        ),
    )(picture, membrane.reshape(sites, atoms), dictionary, momentum)
    return codes.reshape(membrane.shape), new_dictionary, new_momentum


def solution(mesh):
    return jax.shard_map(
        shards,
        mesh=mesh,
        in_specs=(P(None, "row", "col"), P("row", "col", None), P(), P(("row", "col"), None)),
        out_specs=(P("row", "col", None), P(("row", "col"), None), P(("row", "col"), None)),
        check_vma=False,
    )
```

```python
import functools

import jax
import jax.numpy as jnp
from jax import lax
from jax.experimental import pallas as pl
from jax.experimental.pallas import tpu as pltpu
from jax.sharding import PartitionSpec as P

STRIDE = 8
SPAN = 4
MARGIN = SPAN - 1
SWEEPS = 2

THRESHOLD = 0.25
RELAXATION = 0.1
DECAY = 0.9
LEARNING = 0.25
EPSILON = 1e-05

F32 = jnp.float32
BF16 = jnp.bfloat16
MESH = pl.DeviceIdType.MESH


def shrink(potential):
    return potential - jnp.clip(potential, -THRESHOLD, THRESHOLD)


def cells_of(picture):
    channels = picture.shape[0]
    x = picture.reshape(-1, STRIDE, 128)
    y_at = lax.broadcasted_iota(jnp.int32, (1, STRIDE, 128), 1)
    lane = lax.broadcasted_iota(jnp.int32, (1, STRIDE, 128), 2)
    for bit in (1, 2, 4):
        from_later = pltpu.roll(pltpu.roll(x, STRIDE - bit, 1), STRIDE * bit, 2)
        from_earlier = pltpu.roll(pltpu.roll(x, bit, 1), 128 - STRIDE * bit, 2)
        y_bit = (y_at & bit) != 0
        g_bit = (lane & (STRIDE * bit)) != 0
        x = jnp.where(y_bit == g_bit, x, jnp.where(g_bit, from_later, from_earlier))
    x = x.reshape(channels, -1, STRIDE, 128)
    turned = pltpu.roll(x.reshape(-1, STRIDE, 128), 64, 2).reshape(x.shape)
    lower = lane < 64
    left = jnp.concatenate(
        [jnp.where(lower, x[0], turned[1]), jnp.where(lower, turned[0], x[1])], axis=1
    )
    right = jnp.concatenate([x[2], turned[2]], axis=1)
    return jnp.concatenate([left, right[:, :, :64]], axis=2)


def tightened(x):
    n = x.shape[0] // 2
    ends = jnp.concatenate([x[:n, :, 128:], x[n:, :, 128:]], axis=2)
    return jnp.concatenate([x[:, :, :128], ends], axis=0)


def untightened(t):
    n = t.shape[0] * 2 // 3
    ends = jnp.concatenate([t[n:, :, :64], t[n:, :, 64:]], axis=0)
    return jnp.concatenate([t[:n], ends], axis=2)


def peers_of(rows, cols):
    offsets = {(j, 0) for j in range(rows)} | {(0, j) for j in range(0, cols, 2)}
    offsets |= {(j, k % cols) for j in range(rows) for k in (1, -1)}
    return sorted(offsets - {(0, 0)})


def kernel(
    rows, cols,
    picture_ref, membrane_hbm, dictionary_hbm, momentum_hbm,
    codes_out, dictionary_out, momentum_out,
    dic, dic_t, pot, coding, cells_ref, acc, zbuf, cbuf, ext, wide,
    down_out, up_out, t_out, l_out, above_in, below_in, left_in, right_in, corner_in,
    res_ref, edge_ref,
    codes_t, strip_codes, strip_res, strip_edge, share_out, pair_in, summed, share_in,
    momentum_ref, load_sem, spill_send, spill_recv,
    code_send, code_recv, res_send, res_recv, rim_send, rim_recv,
    pair_send, pair_recv, share_send, share_recv,
):
    site_rows, site_cols, cell = cells_ref.shape
    sites, atoms = pot.shape
    patch = dic.shape[1]
    band = patch // SPAN
    pair = band // 2
    scale = patch ** (-0.5)
    share = atoms // rows
    owned = momentum_ref.shape[0]
    me_r, me_c = lax.axis_index("row"), lax.axis_index("col")

    def at(dr, dc):
        return (lax.rem(me_r + dr % rows, rows), lax.rem(me_c + dc % cols, cols))

    def remote(src, dst, send, recv, dr, dc):
        return pltpu.make_async_remote_copy(
            src_ref=src, dst_ref=dst, send_sem=send, recv_sem=recv,
            device_id=at(dr, dc), device_id_type=MESH,
        )

    loads = [
        pltpu.make_async_copy(
            dictionary_hbm.at[:, pl.ds(d * band, band)],
            dic.at[:, pl.ds(d * band, band)],
            load_sem.at[d],
        )
        for d in range(SPAN)
    ]
    membrane_load = pltpu.make_async_copy(membrane_hbm, pot, load_sem.at[SPAN])
    momentum_load = pltpu.make_async_copy(momentum_hbm, momentum_ref, load_sem.at[SPAN + 1])
    for load in [membrane_load] + loads + [momentum_load]:
        load.start()

    barrier = pltpu.get_barrier_semaphore()
    peers = peers_of(rows, cols)
    for dr, dc in peers:
        pl.semaphore_signal(barrier, inc=1, device_id=at(dr, dc), device_id_type=MESH)

    wide[rows * site_rows :] = jnp.zeros((MARGIN, site_cols, band), BF16)
    zbuf[...] = jnp.zeros_like(zbuf)
    cbuf[...] = jnp.zeros_like(cbuf)
    cells_ref[...] = cells_of(picture_ref[...])
    membrane_load.wait()
    coding[...] = shrink(pot[...]).astype(BF16)
    sent = []

    def send(copies):
        for copy in copies:
            copy.start()
        sent.extend(copies)

    sub = lax.broadcasted_iota(jnp.int32, (1, 8, cell), 1)
    low = sub < 4

    def packed(tall):
        n = tall.shape[0] // 2
        split = tall.reshape(n, 2, 8, cell)
        return split[:, 0] + pltpu.roll(split[:, 1], 4, 1)

    def unpacked(tight):
        n = tight.shape[0]
        both = jnp.stack([tight, pltpu.roll(tight, 4, 1)], axis=1)
        return jnp.where(low, both.reshape(2 * n, 8, cell), 0.0)

    def reconstruct(phase, meanwhile):
        for d in range(SPAN):
            if phase == 0:
                loads[d].wait()
            placed = jnp.dot(
                coding[...], dic[:, d * band : (d + 1) * band], preferred_element_type=F32
            ).reshape(site_rows, site_cols, band)
            if d == 0:
                acc[0:site_rows] = placed
            else:
                acc[d : d + site_rows - 1] += placed[: site_rows - 1]
                acc[d + site_rows - 1] = placed[site_rows - 1]
        zbuf[:, 0:site_cols] = acc[:, :, :pair]
        zbuf[:, site_cols:] = jnp.zeros((site_rows + MARGIN, 8, pair), F32)
        zbuf[:, 2 : site_cols + 2] += acc[:, :, pair:]
        every = zbuf[...]
        cbuf[: site_rows + MARGIN] = every[:, :, :cell]
        cbuf[: site_rows + MARGIN, 1 : site_cols + 3] += every[:, : site_cols + 2, cell:]
        ext[...] = cbuf[...] * -scale
        ext[:site_rows, :site_cols] += cells_ref[...]
        beyond = packed(ext[:, site_cols:])
        within = packed(jnp.where(low, ext[:, :8], 0.0))
        tight = lambda part: part.reshape(-1, cell)
        tail, head = slice(site_rows // 2, None), slice(0, 2)
        last = phase == SWEEPS
        t_out[phase] = tight(beyond).astype(BF16)
        down_out[phase] = jnp.concatenate(
            [tight(ext[site_rows : site_rows + MARGIN, :site_cols]), tight(beyond[tail])]
        ).astype(BF16)
        if not last:
            l_out[phase] = tight(within).astype(BF16)
            up_out[phase] = jnp.concatenate(
                [tight(ext[:MARGIN, :site_cols]), tight(beyond[head])]
            ).astype(BF16)
        own_t = site_rows * 4
        main = MARGIN * site_cols
        corner = pl.ds(own_t, 16)

        def hop(k, src, dst, dr, dc):
            return remote(src, dst, spill_send.at[phase, k], spill_recv.at[phase, k], dr, dc)

        if last:
            copies = [
                hop(0, t_out.at[phase, corner], corner_in.at[phase, 0], 1, 1),
                hop(1, down_out.at[phase, pl.ds(0, main)], above_in.at[phase, pl.ds(0, main)], 1, 0),
                hop(2, t_out.at[phase, pl.ds(0, own_t)], left_in.at[phase, pl.ds(0, own_t)], 0, 1),
            ]
        else:
            copies = [
                hop(0, t_out.at[phase, corner], corner_in.at[phase, 0], 1, 1),
                hop(3, l_out.at[phase, pl.ds(0, 16)], corner_in.at[phase, 1], -1, -1),
                hop(4, l_out.at[phase, corner], corner_in.at[phase, 2], 1, -1),
                hop(5, t_out.at[phase, pl.ds(0, 16)], corner_in.at[phase, 3], -1, 1),
                hop(1, down_out.at[phase], above_in.at[phase], 1, 0),
                hop(6, up_out.at[phase], below_in.at[phase], -1, 0),
                hop(2, t_out.at[phase], left_in.at[phase], 0, 1),
                hop(7, l_out.at[phase], right_in.at[phase], 0, -1),
            ]
        if phase == 0:
            pl.semaphore_wait(barrier, len(peers))
        send(copies)
        meanwhile()
        return copies

    has_above, has_below = me_r > 0, me_r < rows - 1
    has_left, has_right = me_c > 0, me_c < cols - 1

    def loose(ref_part):
        return unpacked(ref_part.astype(F32).reshape(-1, 8, cell))

    def gather_spill(phase, copies):
        last = phase == SWEEPS
        for copy in copies:
            copy.wait_recv()
        main = MARGIN * site_cols
        own_t = site_rows * 4
        own, far_r, far_c = slice(0, site_rows), slice(site_rows, None), slice(site_cols, None)
        ext[:MARGIN, :site_cols] += jnp.where(
            has_above, above_in[phase, :main].astype(F32).reshape(MARGIN, site_cols, cell), 0.0
        )
        reach = own_t if last else own_t + 16
        ext[: reach // 4, :8] += jnp.where(has_left, loose(left_in[phase, :reach]), 0.0)
        ext[:SPAN, :8] += jnp.where(
            jnp.logical_and(has_above, has_left), loose(corner_in[phase, 0]), 0.0
        )
        if last:
            return
        ext[far_r, :8] += jnp.where(has_left, loose(corner_in[phase, 3]), 0.0)
        side = ext[:, far_c] + loose(right_in[phase])
        side_head = side[:SPAN] + jnp.where(
            has_above, loose(above_in[phase, main:]) + loose(corner_in[phase, 2]), 0.0
        )
        side_tail = side[site_rows:] + loose(below_in[phase, main:]) + loose(corner_in[phase, 1])
        ext[:, far_c] = jnp.where(has_right, side, 0.0)
        ext[:SPAN, far_c] = jnp.where(has_right, side_head, 0.0)
        ext[far_r, far_c] = jnp.where(jnp.logical_and(has_right, has_below), side_tail, 0.0)
        under = ext[site_rows : site_rows + MARGIN, :site_cols] + below_in[phase, :main].astype(
            F32
        ).reshape(MARGIN, site_cols, cell)
        ext[site_rows : site_rows + MARGIN, :site_cols] = jnp.where(has_below, under, 0.0)

    def widen(n):
        x = ext[:n]
        return jnp.concatenate(
            [x[:, k : k + site_cols] for k in range(SPAN)], axis=2
        ).astype(BF16)

    def turn_dictionary():
        for first in range(0, atoms, 256):
            for d in range(SPAN):
                dic_t[d * band : (d + 1) * band, first : first + 256] = dic[
                    first : first + 256, d * band : (d + 1) * band
                ].T

    for sweep in range(SWEEPS):
        meanwhile = turn_dictionary if sweep == 0 else lambda: None
        gather_spill(sweep, reconstruct(sweep, meanwhile))
        wide[: site_rows + MARGIN] = widen(site_rows + MARGIN)
        last = sweep == SWEEPS - 1
        step = 256 if atoms % 256 == 0 else 128
        for first in range(0, atoms, step):
            drive = jnp.zeros((sites, step), F32)
            for d in range(SPAN):
                drive += jnp.dot(
                    wide[d : d + site_rows].reshape(sites, band),
                    dic_t[d * band : (d + 1) * band, first : first + step],
                    preferred_element_type=F32,
                )
            old = pot[:, first : first + step]
            new = old + RELAXATION * (drive * scale + shrink(old) - old)
            codes = shrink(new)
            coding[:, first : first + step] = codes.astype(BF16)
            if last:
                codes_out[:, first : first + step] = codes
            else:
                pot[:, first : first + step] = new

    def share_of(row):
        return codes_t.at[pl.ds(pl.multiple_of(row * share, share), share)]

    def place_of(row):
        return strip_codes.at[:, pl.ds(pl.multiple_of(row * sites, sites), sites)]

    code_copies = [
        remote(share_of(at(j, 0)[0]), place_of(me_r), code_send.at[j], code_recv.at[j], j, 0)
        for j in range(1, rows)
    ]

    def give_codes():
        codes_t[...] = codes_out[...].T.astype(BF16)
        send(code_copies)
        place_of(me_r)[...] = share_of(me_r)[...]

    gather_spill(SWEEPS, reconstruct(SWEEPS, give_codes))
    residual = ext[:site_rows, :site_cols].astype(BF16).astype(F32)
    res_ref[...] = tightened(residual).astype(BF16)
    left_cols = packed(jnp.where(low, residual[:, :8], 0.0))
    edge_ref[...] = tightened(left_cols).reshape(-1, 128).astype(BF16)
    rim_copies = [
        remote(edge_ref, strip_edge.at[j], rim_send.at[j], rim_recv.at[j], j, -1)
        for j in range(rows)
    ]
    res_copies = [None] + [
        remote(res_ref, strip_res.at[j], res_send.at[j], res_recv.at[j], j, 0)
        for j in range(1, rows)
    ]
    for j in range(rows):
        send([rim_copies[j]] + ([res_copies[j]] if j else []))
    for j in range(rows):
        rim_copies[j].wait_recv()
        if j:
            res_copies[j].wait_recv()
        block = strip_res[j] if j else res_ref[...]
        ext[:site_rows, :site_cols] = untightened(block.astype(F32))
        ext[:site_rows, site_cols:] = jnp.where(has_right, unpacked(untightened(strip_edge[j].astype(F32).reshape(-1, 8, 128))), 0.0)
        source = at(-j, 0)[0]
        wide[pl.ds(source * site_rows, site_rows)] = widen(site_rows)
    for copy in code_copies:
        copy.wait_recv()

    tall = rows * site_rows
    core = lax.rem(me_c, 2)
    chip = lax.div(me_c, 2)
    chips = cols // 2
    twin = (me_r, me_c + 1 - 2 * core)
    pair_copies, share_copies = [], []
    for e in range(2):
        parts = [
            jnp.dot(
                strip_codes[...],
                wide[d : d + tall].reshape(tall * site_cols, band),
                preferred_element_type=F32,
            ).reshape(chips, 2, owned, band)
            for d in (e, e + 2)
        ]
        share_out[e] = jnp.concatenate(parts, axis=2).astype(BF16)
        pair_copies.append(
            pltpu.make_async_remote_copy(
                src_ref=share_out.at[e, :, 1 - core], dst_ref=pair_in.at[e],
                send_sem=pair_send.at[e], recv_sem=pair_recv.at[e],
                device_id=twin, device_id_type=MESH,
            )
        )
        send(pair_copies[e:])
    for e in range(2):
        pair_copies[e].wait_recv()
        summed[e] = (share_out[e, :, core].astype(F32) + pair_in[e].astype(F32)).astype(BF16)
        share_copies.append([
            remote(summed.at[e, lax.rem(chip + j, chips)], share_in.at[e, j],
                   share_send.at[e, j], share_recv.at[e, j], 0, 2 * j)
            for j in range(1, chips)
        ])
        send(share_copies[e])
    momentum_load.wait()
    for e in range(2):
        total = summed[e, chip].astype(F32)
        for j in range(1, chips):
            share_copies[e][j - 1].wait_recv()
            total += share_in[e, j].astype(F32)
        for k in range(2):
            span = pl.ds((e + 2 * k) * band, band)
            momentum_out[:, span] = (
                DECAY * momentum_ref[:, span] + total[k * owned : (k + 1) * owned] * scale
            )
    tile = 2 * owned
    index = me_r * cols + me_c
    first = pl.multiple_of(lax.div(index, 2) * tile, tile)
    both = dic[pl.ds(first, tile)].astype(F32)
    own_atoms = jnp.where(lax.rem(index, 2) == 1, both[owned:], both[:owned])
    weights = own_atoms + LEARNING * momentum_out[...]
    dictionary_out[...] = weights * lax.rsqrt(
        jnp.mean(weights * weights, axis=1, keepdims=True) + EPSILON
    )
    for copy in sent:
        copy.wait_send()


def shards(picture, membrane, dictionary, momentum):
    site_rows, site_cols, atoms = membrane.shape
    sites = site_rows * site_cols
    patch = dictionary.shape[1]
    cell = patch // SPAN // SPAN
    band = patch // SPAN
    owned = momentum.shape[0]
    rows, cols = lax.axis_size("row"), lax.axis_size("col")
    phases = SWEEPS + 1
    vmem, dma = pltpu.VMEM, pltpu.SemaphoreType.DMA
    anywhere = pl.BlockSpec(memory_space=pltpu.HBM)
    in_vmem = pl.BlockSpec(memory_space=pltpu.VMEM)
    codes, new_dictionary, new_momentum = pl.pallas_call(
        functools.partial(kernel, rows, cols),
        out_shape=(
            jax.ShapeDtypeStruct((sites, atoms), F32),
            jax.ShapeDtypeStruct((owned, patch), F32),
            jax.ShapeDtypeStruct((owned, patch), F32),
        ),
        in_specs=[in_vmem, anywhere, anywhere, anywhere],
        out_specs=(in_vmem, in_vmem, in_vmem),
        scratch_shapes=[
            vmem((atoms, patch), BF16),
            vmem((patch, atoms), BF16),
            vmem((sites, atoms), F32),
            vmem((sites, atoms), BF16),
            vmem((site_rows, site_cols, cell), F32),
            vmem((site_rows + MARGIN, site_cols, band), F32),
            vmem((site_rows + MARGIN, site_cols + 8, band // 2), F32),
            vmem((site_rows + SPAN, site_cols + 8, cell), F32),
            vmem((site_rows + SPAN, site_cols + 8, cell), F32),
            vmem((rows * site_rows + MARGIN, site_cols, band), BF16),
            vmem((phases, MARGIN * site_cols + 16, cell), BF16),
            vmem((phases, MARGIN * site_cols + 16, cell), BF16),
            vmem((phases, (site_rows + SPAN) * 4, cell), BF16),
            vmem((phases, (site_rows + SPAN) * 4, cell), BF16),
            vmem((phases, MARGIN * site_cols + 16, cell), BF16),
            vmem((phases, MARGIN * site_cols + 16, cell), BF16),
            vmem((phases, (site_rows + SPAN) * 4, cell), BF16),
            vmem((phases, (site_rows + SPAN) * 4, cell), BF16),
            vmem((phases, 4, 16, cell), BF16),
            vmem((site_rows * 3 // 2, site_cols, 128), BF16),
            vmem((site_rows * 6, 128), BF16),
            vmem((atoms, sites), BF16),
            vmem((atoms // rows, rows * sites), BF16),
            vmem((rows, site_rows * 3 // 2, site_cols, 128), BF16),
            vmem((rows, site_rows * 6, 128), BF16),
            vmem((2, cols // 2, 2, 2 * owned, band), BF16),
            vmem((2, cols // 2, 2 * owned, band), BF16),
            vmem((2, cols // 2, 2 * owned, band), BF16),
            vmem((2, cols // 2, 2 * owned, band), BF16),
            vmem((owned, patch), F32),
            dma((SPAN + 2,)),
            dma((phases, 8)), dma((phases, 8)),
            dma((rows,)), dma((rows,)),
            dma((rows,)), dma((rows,)),
            dma((rows,)), dma((rows,)),
            dma((2,)), dma((2,)),
            dma((2, cols // 2)), dma((2, cols // 2)),
        ],
        compiler_params=pltpu.CompilerParams(
            collective_id=0, has_side_effects=True, vmem_limit_bytes=48 * 2**20
        ),
    )(picture, membrane.reshape(sites, atoms), dictionary, momentum)
    return codes.reshape(membrane.shape), new_dictionary, new_momentum


def solution(mesh):
    return jax.shard_map(
        shards,
        mesh=mesh,
        in_specs=(P(None, "row", "col"), P("row", "col", None), P(), P(("row", "col"), None)),
        out_specs=(P("row", "col", None), P(("row", "col"), None), P(("row", "col"), None)),
        check_vma=False,
    )
```

```python
import functools

import jax
import jax.numpy as jnp
from jax import lax
from jax.experimental import pallas as pl
from jax.experimental.pallas import tpu as pltpu
from jax.sharding import PartitionSpec as P

STRIDE = 8
SPAN = 4
MARGIN = SPAN - 1
SWEEPS = 2

THRESHOLD = 0.25
RELAXATION = 0.1
DECAY = 0.9
LEARNING = 0.25
EPSILON = 1e-05

F32 = jnp.float32
BF16 = jnp.bfloat16
MESH = pl.DeviceIdType.MESH


def shrink(potential):
    return potential - jnp.clip(potential, -THRESHOLD, THRESHOLD)


def cells_of(picture):
    channels = picture.shape[0]
    x = picture.reshape(-1, STRIDE, 128)
    y_at = lax.broadcasted_iota(jnp.int32, (1, STRIDE, 128), 1)
    lane = lax.broadcasted_iota(jnp.int32, (1, STRIDE, 128), 2)
    for bit in (1, 2, 4):
        from_later = pltpu.roll(pltpu.roll(x, STRIDE - bit, 1), STRIDE * bit, 2)
        from_earlier = pltpu.roll(pltpu.roll(x, bit, 1), 128 - STRIDE * bit, 2)
        y_bit = (y_at & bit) != 0
        g_bit = (lane & (STRIDE * bit)) != 0
        x = jnp.where(y_bit == g_bit, x, jnp.where(g_bit, from_later, from_earlier))
    x = x.reshape(channels, -1, STRIDE, 128)
    turned = pltpu.roll(x.reshape(-1, STRIDE, 128), 64, 2).reshape(x.shape)
    lower = lane < 64
    left = jnp.concatenate(
        [jnp.where(lower, x[0], turned[1]), jnp.where(lower, turned[0], x[1])], axis=1
    )
    right = jnp.concatenate([x[2], turned[2]], axis=1)
    return jnp.concatenate([left, right[:, :, :64]], axis=2)


def tightened(x):
    n = x.shape[0] // 2
    ends = jnp.concatenate([x[:n, :, 128:], x[n:, :, 128:]], axis=2)
    return jnp.concatenate([x[:, :, :128], ends], axis=0)


def untightened(t):
    n = t.shape[0] * 2 // 3
    ends = jnp.concatenate([t[n:, :, :64], t[n:, :, 64:]], axis=0)
    return jnp.concatenate([t[:n], ends], axis=2)


def peers_of(rows, cols):
    offsets = {(j, 0) for j in range(rows)} | {(0, j) for j in range(0, cols, 2)}
    offsets |= {(j, k % cols) for j in range(rows) for k in (1, -1)}
    return sorted(offsets - {(0, 0)})


def kernel(
    rows, cols,
    picture_ref, membrane_hbm, dictionary_hbm,
    codes_out, learning_out, atoms_out,
    dic, dic_t, pot, coding, cells_ref, acc, zbuf, cbuf, ext, wide,
    down_out, up_out, t_out, l_out, above_in, below_in, left_in, right_in, corner_in,
    res_ref, edge_ref,
    codes_t, strip_codes, strip_res, strip_edge, share_out, pair_in, summed, share_in,
    load_sem, spill_send, spill_recv,
    code_send, code_recv, res_send, res_recv, rim_send, rim_recv,
    pair_send, pair_recv, share_send, share_recv,
):
    site_rows, site_cols, cell = cells_ref.shape
    sites, atoms = pot.shape
    patch = dic.shape[1]
    band = patch // SPAN
    pair = band // 2
    scale = patch ** (-0.5)
    share = atoms // rows
    owned = learning_out.shape[0]
    me_r, me_c = lax.axis_index("row"), lax.axis_index("col")

    def at(dr, dc):
        return (lax.rem(me_r + dr % rows, rows), lax.rem(me_c + dc % cols, cols))

    def remote(src, dst, send, recv, dr, dc):
        return pltpu.make_async_remote_copy(
            src_ref=src, dst_ref=dst, send_sem=send, recv_sem=recv,
            device_id=at(dr, dc), device_id_type=MESH,
        )

    loads = [
        pltpu.make_async_copy(
            dictionary_hbm.at[:, pl.ds(d * band, band)],
            dic.at[:, pl.ds(d * band, band)],
            load_sem.at[d],
        )
        for d in range(SPAN)
    ]
    membrane_load = pltpu.make_async_copy(membrane_hbm, pot, load_sem.at[SPAN])
    for load in [membrane_load] + loads:
        load.start()

    barrier = pltpu.get_barrier_semaphore()
    peers = peers_of(rows, cols)
    for dr, dc in peers:
        pl.semaphore_signal(barrier, inc=1, device_id=at(dr, dc), device_id_type=MESH)

    wide[rows * site_rows :] = jnp.zeros((MARGIN, site_cols, band), BF16)
    zbuf[...] = jnp.zeros_like(zbuf)
    cbuf[...] = jnp.zeros_like(cbuf)
    cells_ref[...] = cells_of(picture_ref[...])
    membrane_load.wait()
    coding[...] = shrink(pot[...]).astype(BF16)
    sent = []

    def send(copies):
        for copy in copies:
            copy.start()
        sent.extend(copies)

    def settle(keep=0):
        while len(sent) > keep:
            sent.pop(0).wait_send()

    sub = lax.broadcasted_iota(jnp.int32, (1, 8, cell), 1)
    low = sub < 4

    def packed(tall):
        n = tall.shape[0] // 2
        split = tall.reshape(n, 2, 8, cell)
        return split[:, 0] + pltpu.roll(split[:, 1], 4, 1)

    def unpacked(tight):
        n = tight.shape[0]
        both = jnp.stack([tight, pltpu.roll(tight, 4, 1)], axis=1)
        return jnp.where(low, both.reshape(2 * n, 8, cell), 0.0)

    def reconstruct(phase, meanwhile):
        for d in range(SPAN):
            if phase == 0:
                loads[d].wait()
            placed = jnp.dot(
                coding[...], dic[:, d * band : (d + 1) * band], preferred_element_type=F32
            ).reshape(site_rows, site_cols, band)
            if d == 0:
                acc[0:site_rows] = placed
            else:
                acc[d : d + site_rows - 1] += placed[: site_rows - 1]
                acc[d + site_rows - 1] = placed[site_rows - 1]
        zbuf[:, 0:site_cols] = acc[:, :, :pair]
        zbuf[:, site_cols:] = jnp.zeros((site_rows + MARGIN, 8, pair), F32)
        zbuf[:, 2 : site_cols + 2] += acc[:, :, pair:]
        every = zbuf[...]
        cbuf[: site_rows + MARGIN] = every[:, :, :cell]
        cbuf[: site_rows + MARGIN, 1 : site_cols + 3] += every[:, : site_cols + 2, cell:]
        ext[...] = cbuf[...] * -scale
        ext[:site_rows, :site_cols] += cells_ref[...]
        beyond = packed(ext[:, site_cols:])
        within = packed(jnp.where(low, ext[:, :8], 0.0))
        tight = lambda part: part.reshape(-1, cell)
        tail, head = slice(site_rows // 2, None), slice(0, 2)
        last = phase == SWEEPS
        t_out[phase] = tight(beyond).astype(BF16)
        down_out[phase] = jnp.concatenate(
            [tight(ext[site_rows : site_rows + MARGIN, :site_cols]), tight(beyond[tail])]
        ).astype(BF16)
        if not last:
            l_out[phase] = tight(within).astype(BF16)
            up_out[phase] = jnp.concatenate(
                [tight(ext[:MARGIN, :site_cols]), tight(beyond[head])]
            ).astype(BF16)
        own_t = site_rows * 4
        main = MARGIN * site_cols
        corner = pl.ds(own_t, 16)

        def hop(k, src, dst, dr, dc):
            return remote(src, dst, spill_send.at[phase, k], spill_recv.at[phase, k], dr, dc)

        if last:
            copies = [
                hop(0, t_out.at[phase, corner], corner_in.at[phase, 0], 1, 1),
                hop(1, down_out.at[phase, pl.ds(0, main)], above_in.at[phase, pl.ds(0, main)], 1, 0),
                hop(2, t_out.at[phase, pl.ds(0, own_t)], left_in.at[phase, pl.ds(0, own_t)], 0, 1),
            ]
        else:
            copies = [
                hop(0, t_out.at[phase, corner], corner_in.at[phase, 0], 1, 1),
                hop(3, l_out.at[phase, pl.ds(0, 16)], corner_in.at[phase, 1], -1, -1),
                hop(4, l_out.at[phase, corner], corner_in.at[phase, 2], 1, -1),
                hop(5, t_out.at[phase, pl.ds(0, 16)], corner_in.at[phase, 3], -1, 1),
                hop(1, down_out.at[phase], above_in.at[phase], 1, 0),
                hop(6, up_out.at[phase], below_in.at[phase], -1, 0),
                hop(2, t_out.at[phase], left_in.at[phase], 0, 1),
                hop(7, l_out.at[phase], right_in.at[phase], 0, -1),
            ]
        if phase == 0:
            pl.semaphore_wait(barrier, len(peers))
        send(copies)
        meanwhile()
        settle(len(copies) + (rows - 1 if last else 0))
        return copies

    has_above, has_below = me_r > 0, me_r < rows - 1
    has_left, has_right = me_c > 0, me_c < cols - 1

    def loose(ref_part):
        return unpacked(ref_part.astype(F32).reshape(-1, 8, cell))

    def gather_spill(phase, copies):
        last = phase == SWEEPS
        for copy in copies:
            copy.wait_recv()
        main = MARGIN * site_cols
        own_t = site_rows * 4
        own, far_r, far_c = slice(0, site_rows), slice(site_rows, None), slice(site_cols, None)
        ext[:MARGIN, :site_cols] += jnp.where(
            has_above, above_in[phase, :main].astype(F32).reshape(MARGIN, site_cols, cell), 0.0
        )
        reach = own_t if last else own_t + 16
        ext[: reach // 4, :8] += jnp.where(has_left, loose(left_in[phase, :reach]), 0.0)
        ext[:SPAN, :8] += jnp.where(
            jnp.logical_and(has_above, has_left), loose(corner_in[phase, 0]), 0.0
        )
        if last:
            return
        ext[far_r, :8] += jnp.where(has_left, loose(corner_in[phase, 3]), 0.0)
        side = ext[:, far_c] + loose(right_in[phase])
        side_head = side[:SPAN] + jnp.where(
            has_above, loose(above_in[phase, main:]) + loose(corner_in[phase, 2]), 0.0
        )
        side_tail = side[site_rows:] + loose(below_in[phase, main:]) + loose(corner_in[phase, 1])
        ext[:, far_c] = jnp.where(has_right, side, 0.0)
        ext[:SPAN, far_c] = jnp.where(has_right, side_head, 0.0)
        ext[far_r, far_c] = jnp.where(jnp.logical_and(has_right, has_below), side_tail, 0.0)
        under = ext[site_rows : site_rows + MARGIN, :site_cols] + below_in[phase, :main].astype(
            F32
        ).reshape(MARGIN, site_cols, cell)
        ext[site_rows : site_rows + MARGIN, :site_cols] = jnp.where(has_below, under, 0.0)

    def widen(n):
        x = ext[:n]
        return jnp.concatenate(
            [x[:, k : k + site_cols] for k in range(SPAN)], axis=2
        ).astype(BF16)

    def turn_dictionary():
        for first in range(0, atoms, 256):
            for d in range(SPAN):
                dic_t[d * band : (d + 1) * band, first : first + 256] = dic[
                    first : first + 256, d * band : (d + 1) * band
                ].T

    for sweep in range(SWEEPS):
        meanwhile = turn_dictionary if sweep == 0 else lambda: None
        gather_spill(sweep, reconstruct(sweep, meanwhile))
        wide[: site_rows + MARGIN] = widen(site_rows + MARGIN)
        last = sweep == SWEEPS - 1
        step = 256 if atoms % 256 == 0 else 128
        for first in range(0, atoms, step):
            drive = jnp.zeros((sites, step), F32)
            for d in range(SPAN):
                drive += jnp.dot(
                    wide[d : d + site_rows].reshape(sites, band),
                    dic_t[d * band : (d + 1) * band, first : first + step],
                    preferred_element_type=F32,
                )
            old = pot[:, first : first + step]
            new = old + RELAXATION * (drive * scale + shrink(old) - old)
            codes = shrink(new)
            coding[:, first : first + step] = codes.astype(BF16)
            if last:
                codes_out[:, first : first + step] = codes
            else:
                pot[:, first : first + step] = new

    def share_of(row):
        return codes_t.at[pl.ds(pl.multiple_of(row * share, share), share)]

    def place_of(row):
        return strip_codes.at[:, pl.ds(pl.multiple_of(row * sites, sites), sites)]

    code_copies = [
        remote(share_of(at(j, 0)[0]), place_of(me_r), code_send.at[j], code_recv.at[j], j, 0)
        for j in range(1, rows)
    ]

    def give_codes():
        codes_t[...] = codes_out[...].T.astype(BF16)
        send(code_copies)
        place_of(me_r)[...] = share_of(me_r)[...]

    gather_spill(SWEEPS, reconstruct(SWEEPS, give_codes))
    residual = ext[:site_rows, :site_cols].astype(BF16).astype(F32)
    res_ref[...] = tightened(residual).astype(BF16)
    left_cols = packed(jnp.where(low, residual[:, :8], 0.0))
    edge_ref[...] = tightened(left_cols).reshape(-1, 128).astype(BF16)
    rim_copies = [
        remote(edge_ref, strip_edge.at[j], rim_send.at[j], rim_recv.at[j], j, -1)
        for j in range(rows)
    ]
    res_copies = [None] + [
        remote(res_ref, strip_res.at[j], res_send.at[j], res_recv.at[j], j, 0)
        for j in range(1, rows)
    ]
    for j in range(rows):
        send([rim_copies[j]] + ([res_copies[j]] if j else []))
    settle(2 * rows - 1)
    for j in range(rows):
        rim_copies[j].wait_recv()
        if j:
            res_copies[j].wait_recv()
        block = strip_res[j] if j else res_ref[...]
        ext[:site_rows, :site_cols] = untightened(block.astype(F32))
        ext[:site_rows, site_cols:] = jnp.where(has_right, unpacked(untightened(strip_edge[j].astype(F32).reshape(-1, 8, 128))), 0.0)
        source = at(-j, 0)[0]
        wide[pl.ds(source * site_rows, site_rows)] = widen(site_rows)
    for copy in code_copies:
        copy.wait_recv()

    tall = rows * site_rows
    core = lax.rem(me_c, 2)
    chip = lax.div(me_c, 2)
    chips = cols // 2
    twin = (me_r, me_c + 1 - 2 * core)
    pair_copies, share_copies = [], []
    for e in range(2):
        parts = [
            jnp.dot(
                strip_codes[...],
                wide[d : d + tall].reshape(tall * site_cols, band),
                preferred_element_type=F32,
            ).reshape(chips, 2, owned, band)
            for d in (e, e + 2)
        ]
        share_out[e] = jnp.concatenate(parts, axis=2).astype(BF16)
        pair_copies.append(
            pltpu.make_async_remote_copy(
                src_ref=share_out.at[e, :, 1 - core], dst_ref=pair_in.at[e],
                send_sem=pair_send.at[e], recv_sem=pair_recv.at[e],
                device_id=twin, device_id_type=MESH,
            )
        )
        send(pair_copies[e:])
    for e in range(2):
        pair_copies[e].wait_recv()
        summed[e] = (share_out[e, :, core].astype(F32) + pair_in[e].astype(F32)).astype(BF16)
        share_copies.append([
            remote(summed.at[e, lax.rem(chip + j, chips)], share_in.at[e, j],
                   share_send.at[e, j], share_recv.at[e, j], 0, 2 * j)
            for j in range(1, chips)
        ])
        send(share_copies[e])
    settle(2 * (chips - 1))
    for e in range(2):
        total = summed[e, chip].astype(F32)
        for j in range(1, chips):
            share_copies[e][j - 1].wait_recv()
            total += share_in[e, j].astype(F32)
        for k in range(2):
            span = pl.ds((e + 2 * k) * band, band)
            learning_out[:, span] = total[k * owned : (k + 1) * owned] * scale
    tile = 2 * owned
    index = me_r * cols + me_c
    first = pl.multiple_of(lax.div(index, 2) * tile, tile)
    both = dic[pl.ds(first, tile)].astype(F32)
    atoms_out[...] = jnp.where(lax.rem(index, 2) == 1, both[owned:], both[:owned])
    settle()


def finish(
    codes_ref, learning_ref, atoms_ref, momentum_ref,
    codes_out, dictionary_out, momentum_out, sem,
):
    codes_copy = pltpu.make_async_copy(codes_ref, codes_out, sem)
    codes_copy.start()
    momentum = DECAY * momentum_ref[...] + learning_ref[...]
    weights = atoms_ref[...] + LEARNING * momentum
    momentum_out[...] = momentum
    dictionary_out[...] = weights * lax.rsqrt(
        jnp.mean(weights * weights, axis=1, keepdims=True) + EPSILON
    )
    codes_copy.wait()


def shards(picture, membrane, dictionary, momentum):
    site_rows, site_cols, atoms = membrane.shape
    sites = site_rows * site_cols
    patch = dictionary.shape[1]
    cell = patch // SPAN // SPAN
    band = patch // SPAN
    owned = momentum.shape[0]
    rows, cols = lax.axis_size("row"), lax.axis_size("col")
    phases = SWEEPS + 1
    vmem, dma = pltpu.VMEM, pltpu.SemaphoreType.DMA
    anywhere = pl.BlockSpec(memory_space=pltpu.HBM)
    in_vmem = pl.BlockSpec(memory_space=pltpu.VMEM)
    results = pl.pallas_call(
        functools.partial(kernel, rows, cols),
        out_shape=(
            jax.ShapeDtypeStruct((sites, atoms), F32),
            jax.ShapeDtypeStruct((owned, patch), F32),
            jax.ShapeDtypeStruct((owned, patch), F32),
        ),
        in_specs=[in_vmem, anywhere, anywhere],
        out_specs=(in_vmem, in_vmem, in_vmem),
        scratch_shapes=[
            vmem((atoms, patch), BF16),
            vmem((patch, atoms), BF16),
            vmem((sites, atoms), F32),
            vmem((sites, atoms), BF16),
            vmem((site_rows, site_cols, cell), F32),
            vmem((site_rows + MARGIN, site_cols, band), F32),
            vmem((site_rows + MARGIN, site_cols + 8, band // 2), F32),
            vmem((site_rows + SPAN, site_cols + 8, cell), F32),
            vmem((site_rows + SPAN, site_cols + 8, cell), F32),
            vmem((rows * site_rows + MARGIN, site_cols, band), BF16),
            vmem((phases, MARGIN * site_cols + 16, cell), BF16),
            vmem((phases, MARGIN * site_cols + 16, cell), BF16),
            vmem((phases, (site_rows + SPAN) * 4, cell), BF16),
            vmem((phases, (site_rows + SPAN) * 4, cell), BF16),
            vmem((phases, MARGIN * site_cols + 16, cell), BF16),
            vmem((phases, MARGIN * site_cols + 16, cell), BF16),
            vmem((phases, (site_rows + SPAN) * 4, cell), BF16),
            vmem((phases, (site_rows + SPAN) * 4, cell), BF16),
            vmem((phases, 4, 16, cell), BF16),
            vmem((site_rows * 3 // 2, site_cols, 128), BF16),
            vmem((site_rows * 6, 128), BF16),
            vmem((atoms, sites), BF16),
            vmem((atoms // rows, rows * sites), BF16),
            vmem((rows, site_rows * 3 // 2, site_cols, 128), BF16),
            vmem((rows, site_rows * 6, 128), BF16),
            vmem((2, cols // 2, 2, 2 * owned, band), BF16),
            vmem((2, cols // 2, 2 * owned, band), BF16),
            vmem((2, cols // 2, 2 * owned, band), BF16),
            vmem((2, cols // 2, 2 * owned, band), BF16),
            dma((SPAN + 1,)),
            dma((phases, 8)), dma((phases, 8)),
            dma((rows,)), dma((rows,)),
            dma((rows,)), dma((rows,)),
            dma((rows,)), dma((rows,)),
            dma((2,)), dma((2,)),
            dma((2, cols // 2)), dma((2, cols // 2)),
        ],
        compiler_params=pltpu.CompilerParams(
            collective_id=0, has_side_effects=True, vmem_limit_bytes=48 * 2**20
        ),
    )(picture, membrane.reshape(sites, atoms), dictionary)
    codes, new_dictionary, new_momentum = pl.pallas_call(
        finish,
        out_shape=tuple(jax.ShapeDtypeStruct(x.shape, x.dtype) for x in results),
        in_specs=[in_vmem] * 4,
        out_specs=(anywhere, in_vmem, in_vmem),
        scratch_shapes=[dma(())],
        compiler_params=pltpu.CompilerParams(vmem_limit_bytes=4 * 2**20),
    )(*results, momentum)
    return codes.reshape(membrane.shape), new_dictionary, new_momentum


def solution(mesh):
    return jax.shard_map(
        shards,
        mesh=mesh,
        in_specs=(P(None, "row", "col"), P("row", "col", None), P(), P(("row", "col"), None)),
        out_specs=(P("row", "col", None), P(("row", "col"), None), P(("row", "col"), None)),
        check_vma=False,
    )
```

```python
import functools

import jax
import jax.numpy as jnp
from jax import lax
from jax.experimental import pallas as pl
from jax.experimental.pallas import tpu as pltpu
from jax.sharding import PartitionSpec as P

STRIDE = 8
SPAN = 4
MARGIN = SPAN - 1
SWEEPS = 2

THRESHOLD = 0.25
RELAXATION = 0.1
DECAY = 0.9
LEARNING = 0.25
EPSILON = 1e-05

F32 = jnp.float32
BF16 = jnp.bfloat16
MESH = pl.DeviceIdType.MESH


def shrink(potential):
    return potential - jnp.clip(potential, -THRESHOLD, THRESHOLD)


def cells_of(picture):
    channels = picture.shape[0]
    x = picture.reshape(-1, STRIDE, 128)
    y_at = lax.broadcasted_iota(jnp.int32, (1, STRIDE, 128), 1)
    lane = lax.broadcasted_iota(jnp.int32, (1, STRIDE, 128), 2)
    for bit in (1, 2, 4):
        from_later = pltpu.roll(pltpu.roll(x, STRIDE - bit, 1), STRIDE * bit, 2)
        from_earlier = pltpu.roll(pltpu.roll(x, bit, 1), 128 - STRIDE * bit, 2)
        y_bit = (y_at & bit) != 0
        g_bit = (lane & (STRIDE * bit)) != 0
        x = jnp.where(y_bit == g_bit, x, jnp.where(g_bit, from_later, from_earlier))
    x = x.reshape(channels, -1, STRIDE, 128)
    turned = pltpu.roll(x.reshape(-1, STRIDE, 128), 64, 2).reshape(x.shape)
    lower = lane < 64
    left = jnp.concatenate(
        [jnp.where(lower, x[0], turned[1]), jnp.where(lower, turned[0], x[1])], axis=1
    )
    right = jnp.concatenate([x[2], turned[2]], axis=1)
    return jnp.concatenate([left, right[:, :, :64]], axis=2)


def tightened(x):
    n = x.shape[0] // 2
    ends = jnp.concatenate([x[:n, :, 128:], x[n:, :, 128:]], axis=2)
    return jnp.concatenate([x[:, :, :128], ends], axis=0)


def untightened(t):
    n = t.shape[0] * 2 // 3
    ends = jnp.concatenate([t[n:, :, :64], t[n:, :, 64:]], axis=0)
    return jnp.concatenate([t[:n], ends], axis=2)


def peers_of(rows, cols):
    offsets = {(j, 0) for j in range(rows)} | {(0, j) for j in range(0, cols, 2)}
    offsets |= {(j, k % cols) for j in range(rows) for k in (1, -1)}
    return sorted(offsets - {(0, 0)})


def kernel(
    rows, cols,
    picture_hbm, membrane_hbm, dictionary_hbm,
    codes_out, learning_out, atoms_out,
    picture_ref, dic, dic_t, pot, coding, cells_ref, acc, zbuf, cbuf, ext, wide,
    down_out, up_out, t_out, l_out, above_in, below_in, left_in, right_in, corner_in,
    res_ref, edge_ref,
    codes_t, strip_codes, strip_res, strip_edge, share_out, pair_in, summed, share_in,
    load_sem, spill_send, spill_recv,
    code_send, code_recv, res_send, res_recv, rim_send, rim_recv,
    pair_send, pair_recv, share_send, share_recv,
):
    site_rows, site_cols, cell = cells_ref.shape
    sites, atoms = pot.shape
    patch = dic.shape[1]
    band = patch // SPAN
    pair = band // 2
    scale = patch ** (-0.5)
    share = atoms // rows
    owned = learning_out.shape[0]
    me_r, me_c = lax.axis_index("row"), lax.axis_index("col")

    def at(dr, dc):
        return (lax.rem(me_r + dr % rows, rows), lax.rem(me_c + dc % cols, cols))

    def remote(src, dst, send, recv, dr, dc):
        return pltpu.make_async_remote_copy(
            src_ref=src, dst_ref=dst, send_sem=send, recv_sem=recv,
            device_id=at(dr, dc), device_id_type=MESH,
        )

    loads = [
        pltpu.make_async_copy(
            dictionary_hbm.at[:, pl.ds(d * band, band)],
            dic.at[:, pl.ds(d * band, band)],
            load_sem.at[d],
        )
        for d in range(SPAN)
    ]
    membrane_load = pltpu.make_async_copy(membrane_hbm, pot, load_sem.at[SPAN])
    picture_load = pltpu.make_async_copy(picture_hbm, picture_ref, load_sem.at[SPAN + 1])
    for load in [membrane_load] + loads[:1] + [picture_load] + loads[1:]:
        load.start()

    barrier = pltpu.get_barrier_semaphore()
    peers = peers_of(rows, cols)
    for dr, dc in peers:
        pl.semaphore_signal(barrier, inc=1, device_id=at(dr, dc), device_id_type=MESH)

    wide[rows * site_rows :] = jnp.zeros((MARGIN, site_cols, band), BF16)
    zbuf[...] = jnp.zeros_like(zbuf)
    cbuf[...] = jnp.zeros_like(cbuf)
    membrane_load.wait()
    coding[...] = shrink(pot[...]).astype(BF16)
    sent = []

    def send(copies):
        for copy in copies:
            copy.start()
        sent.extend(copies)

    def settle(keep=0):
        while len(sent) > keep:
            sent.pop(0).wait_send()

    sub = lax.broadcasted_iota(jnp.int32, (1, 8, cell), 1)
    low = sub < 4

    def packed(tall):
        n = tall.shape[0] // 2
        split = tall.reshape(n, 2, 8, cell)
        return split[:, 0] + pltpu.roll(split[:, 1], 4, 1)

    def unpacked(tight):
        n = tight.shape[0]
        both = jnp.stack([tight, pltpu.roll(tight, 4, 1)], axis=1)
        return jnp.where(low, both.reshape(2 * n, 8, cell), 0.0)

    def reconstruct(phase, meanwhile):
        for d in range(SPAN):
            if phase == 0:
                loads[d].wait()
            placed = jnp.dot(
                coding[...], dic[:, d * band : (d + 1) * band], preferred_element_type=F32
            ).reshape(site_rows, site_cols, band)
            if d == 0:
                acc[0:site_rows] = placed
            else:
                acc[d : d + site_rows - 1] += placed[: site_rows - 1]
                acc[d + site_rows - 1] = placed[site_rows - 1]
        zbuf[:, 0:site_cols] = acc[:, :, :pair]
        zbuf[:, site_cols:] = jnp.zeros((site_rows + MARGIN, 8, pair), F32)
        zbuf[:, 2 : site_cols + 2] += acc[:, :, pair:]
        every = zbuf[...]
        cbuf[: site_rows + MARGIN] = every[:, :, :cell]
        cbuf[: site_rows + MARGIN, 1 : site_cols + 3] += every[:, : site_cols + 2, cell:]
        ext[...] = cbuf[...] * -scale
        if phase == 0:
            picture_load.wait()
            cells_ref[...] = cells_of(picture_ref[...])
        ext[:site_rows, :site_cols] += cells_ref[...]
        beyond = packed(ext[:, site_cols:])
        within = packed(jnp.where(low, ext[:, :8], 0.0))
        tight = lambda part: part.reshape(-1, cell)
        tail, head = slice(site_rows // 2, None), slice(0, 2)
        last = phase == SWEEPS
        t_out[phase] = tight(beyond).astype(BF16)
        down_out[phase] = jnp.concatenate(
            [tight(ext[site_rows : site_rows + MARGIN, :site_cols]), tight(beyond[tail])]
        ).astype(BF16)
        if not last:
            l_out[phase] = tight(within).astype(BF16)
            up_out[phase] = jnp.concatenate(
                [tight(ext[:MARGIN, :site_cols]), tight(beyond[head])]
            ).astype(BF16)
        own_t = site_rows * 4
        main = MARGIN * site_cols
        corner = pl.ds(own_t, 16)

        def hop(k, src, dst, dr, dc):
            return remote(src, dst, spill_send.at[phase, k], spill_recv.at[phase, k], dr, dc)

        if last:
            copies = [
                hop(0, t_out.at[phase, corner], corner_in.at[phase, 0], 1, 1),
                hop(1, down_out.at[phase, pl.ds(0, main)], above_in.at[phase, pl.ds(0, main)], 1, 0),
                hop(2, t_out.at[phase, pl.ds(0, own_t)], left_in.at[phase, pl.ds(0, own_t)], 0, 1),
            ]
        else:
            copies = [
                hop(0, t_out.at[phase, corner], corner_in.at[phase, 0], 1, 1),
                hop(3, l_out.at[phase, pl.ds(0, 16)], corner_in.at[phase, 1], -1, -1),
                hop(4, l_out.at[phase, corner], corner_in.at[phase, 2], 1, -1),
                hop(5, t_out.at[phase, pl.ds(0, 16)], corner_in.at[phase, 3], -1, 1),
                hop(1, down_out.at[phase], above_in.at[phase], 1, 0),
                hop(6, up_out.at[phase], below_in.at[phase], -1, 0),
                hop(2, t_out.at[phase], left_in.at[phase], 0, 1),
                hop(7, l_out.at[phase], right_in.at[phase], 0, -1),
            ]
        if phase == 0:
            pl.semaphore_wait(barrier, len(peers))
        send(copies)
        meanwhile()
        settle(len(copies) + (rows - 1 if last else 0))
        return copies

    has_above, has_below = me_r > 0, me_r < rows - 1
    has_left, has_right = me_c > 0, me_c < cols - 1

    def loose(ref_part):
        return unpacked(ref_part.astype(F32).reshape(-1, 8, cell))

    def gather_spill(phase, copies):
        last = phase == SWEEPS
        for copy in copies:
            copy.wait_recv()
        main = MARGIN * site_cols
        own_t = site_rows * 4
        own, far_r, far_c = slice(0, site_rows), slice(site_rows, None), slice(site_cols, None)
        ext[:MARGIN, :site_cols] += jnp.where(
            has_above, above_in[phase, :main].astype(F32).reshape(MARGIN, site_cols, cell), 0.0
        )
        reach = own_t if last else own_t + 16
        ext[: reach // 4, :8] += jnp.where(has_left, loose(left_in[phase, :reach]), 0.0)
        ext[:SPAN, :8] += jnp.where(
            jnp.logical_and(has_above, has_left), loose(corner_in[phase, 0]), 0.0
        )
        if last:
            return
        ext[far_r, :8] += jnp.where(has_left, loose(corner_in[phase, 3]), 0.0)
        side = ext[:, far_c] + loose(right_in[phase])
        side_head = side[:SPAN] + jnp.where(
            has_above, loose(above_in[phase, main:]) + loose(corner_in[phase, 2]), 0.0
        )
        side_tail = side[site_rows:] + loose(below_in[phase, main:]) + loose(corner_in[phase, 1])
        ext[:, far_c] = jnp.where(has_right, side, 0.0)
        ext[:SPAN, far_c] = jnp.where(has_right, side_head, 0.0)
        ext[far_r, far_c] = jnp.where(jnp.logical_and(has_right, has_below), side_tail, 0.0)
        under = ext[site_rows : site_rows + MARGIN, :site_cols] + below_in[phase, :main].astype(
            F32
        ).reshape(MARGIN, site_cols, cell)
        ext[site_rows : site_rows + MARGIN, :site_cols] = jnp.where(has_below, under, 0.0)

    def widen(n):
        x = ext[:n]
        return jnp.concatenate(
            [x[:, k : k + site_cols] for k in range(SPAN)], axis=2
        ).astype(BF16)

    def turn_dictionary():
        for first in range(0, atoms, 256):
            for d in range(SPAN):
                dic_t[d * band : (d + 1) * band, first : first + 256] = dic[
                    first : first + 256, d * band : (d + 1) * band
                ].T

    for sweep in range(SWEEPS):
        meanwhile = turn_dictionary if sweep == 0 else lambda: None
        gather_spill(sweep, reconstruct(sweep, meanwhile))
        wide[: site_rows + MARGIN] = widen(site_rows + MARGIN)
        last = sweep == SWEEPS - 1
        step = 256 if atoms % 256 == 0 else 128
        for first in range(0, atoms, step):
            drive = jnp.zeros((sites, step), F32)
            for d in range(SPAN):
                drive += jnp.dot(
                    wide[d : d + site_rows].reshape(sites, band),
                    dic_t[d * band : (d + 1) * band, first : first + step],
                    preferred_element_type=F32,
                )
            old = pot[:, first : first + step]
            new = old + RELAXATION * (drive * scale + shrink(old) - old)
            codes = shrink(new)
            coding[:, first : first + step] = codes.astype(BF16)
            if last:
                codes_out[:, first : first + step] = codes
            else:
                pot[:, first : first + step] = new

    def share_of(row):
        return codes_t.at[pl.ds(pl.multiple_of(row * share, share), share)]

    def place_of(row):
        return strip_codes.at[:, pl.ds(pl.multiple_of(row * sites, sites), sites)]

    code_copies = [
        remote(share_of(at(j, 0)[0]), place_of(me_r), code_send.at[j], code_recv.at[j], j, 0)
        for j in range(1, rows)
    ]

    def give_codes():
        codes_t[...] = codes_out[...].T.astype(BF16)
        send(code_copies)
        place_of(me_r)[...] = share_of(me_r)[...]

    gather_spill(SWEEPS, reconstruct(SWEEPS, give_codes))
    residual = ext[:site_rows, :site_cols].astype(BF16).astype(F32)
    res_ref[...] = tightened(residual).astype(BF16)
    left_cols = packed(jnp.where(low, residual[:, :8], 0.0))
    edge_ref[...] = tightened(left_cols).reshape(-1, 128).astype(BF16)
    rim_copies = [
        remote(edge_ref, strip_edge.at[j], rim_send.at[j], rim_recv.at[j], j, -1)
        for j in range(rows)
    ]
    res_copies = [None] + [
        remote(res_ref, strip_res.at[j], res_send.at[j], res_recv.at[j], j, 0)
        for j in range(1, rows)
    ]
    for j in range(rows):
        send([rim_copies[j]] + ([res_copies[j]] if j else []))
    settle(2 * rows - 1)
    for j in range(rows):
        rim_copies[j].wait_recv()
        if j:
            res_copies[j].wait_recv()
        block = strip_res[j] if j else res_ref[...]
        ext[:site_rows, :site_cols] = untightened(block.astype(F32))
        ext[:site_rows, site_cols:] = jnp.where(has_right, unpacked(untightened(strip_edge[j].astype(F32).reshape(-1, 8, 128))), 0.0)
        source = at(-j, 0)[0]
        wide[pl.ds(source * site_rows, site_rows)] = widen(site_rows)
    for copy in code_copies:
        copy.wait_recv()

    tall = rows * site_rows
    core = lax.rem(me_c, 2)
    chip = lax.div(me_c, 2)
    chips = cols // 2
    twin = (me_r, me_c + 1 - 2 * core)
    pair_copies, share_copies = [], []
    for e in range(2):
        parts = [
            jnp.dot(
                strip_codes[...],
                wide[d : d + tall].reshape(tall * site_cols, band),
                preferred_element_type=F32,
            ).reshape(chips, 2, owned, band)
            for d in (e, e + 2)
        ]
        share_out[e] = jnp.concatenate(parts, axis=2).astype(BF16)
        pair_copies.append(
            pltpu.make_async_remote_copy(
                src_ref=share_out.at[e, :, 1 - core], dst_ref=pair_in.at[e],
                send_sem=pair_send.at[e], recv_sem=pair_recv.at[e],
                device_id=twin, device_id_type=MESH,
            )
        )
        send(pair_copies[e:])
    for e in range(2):
        pair_copies[e].wait_recv()
        summed[e] = (share_out[e, :, core].astype(F32) + pair_in[e].astype(F32)).astype(BF16)
    share_copies = [
        remote(summed.at[:, lax.rem(chip + j, chips)], share_in.at[:, j],
               share_send.at[0, j], share_recv.at[0, j], 0, 2 * j)
        for j in range(1, chips)
    ]
    send(share_copies)
    settle(chips - 1)
    for copy in share_copies:
        copy.wait_recv()
    for e in range(2):
        total = summed[e, chip].astype(F32)
        for j in range(1, chips):
            total += share_in[e, j].astype(F32)
        for k in range(2):
            span = pl.ds((e + 2 * k) * band, band)
            learning_out[:, span] = total[k * owned : (k + 1) * owned] * scale
    tile = 2 * owned
    index = me_r * cols + me_c
    first = pl.multiple_of(lax.div(index, 2) * tile, tile)
    both = dic[pl.ds(first, tile)].astype(F32)
    atoms_out[...] = jnp.where(lax.rem(index, 2) == 1, both[owned:], both[:owned])
    settle()


def finish(
    codes_ref, learning_ref, atoms_ref, momentum_ref,
    codes_out, dictionary_out, momentum_out, sem,
):
    codes_copy = pltpu.make_async_copy(codes_ref, codes_out, sem)
    codes_copy.start()
    momentum = DECAY * momentum_ref[...] + learning_ref[...]
    weights = atoms_ref[...] + LEARNING * momentum
    momentum_out[...] = momentum
    dictionary_out[...] = weights * lax.rsqrt(
        jnp.mean(weights * weights, axis=1, keepdims=True) + EPSILON
    )
    codes_copy.wait()


def shards(picture, membrane, dictionary, momentum):
    site_rows, site_cols, atoms = membrane.shape
    sites = site_rows * site_cols
    patch = dictionary.shape[1]
    cell = patch // SPAN // SPAN
    band = patch // SPAN
    owned = momentum.shape[0]
    rows, cols = lax.axis_size("row"), lax.axis_size("col")
    phases = SWEEPS + 1
    vmem, dma = pltpu.VMEM, pltpu.SemaphoreType.DMA
    anywhere = pl.BlockSpec(memory_space=pltpu.HBM)
    in_vmem = pl.BlockSpec(memory_space=pltpu.VMEM)
    results = pl.pallas_call(
        functools.partial(kernel, rows, cols),
        out_shape=(
            jax.ShapeDtypeStruct((sites, atoms), F32),
            jax.ShapeDtypeStruct((owned, patch), F32),
            jax.ShapeDtypeStruct((owned, patch), F32),
        ),
        in_specs=[anywhere, anywhere, anywhere],
        out_specs=(in_vmem, in_vmem, in_vmem),
        scratch_shapes=[
            vmem(picture.shape, F32),
            vmem((atoms, patch), BF16),
            vmem((patch, atoms), BF16),
            vmem((sites, atoms), F32),
            vmem((sites, atoms), BF16),
            vmem((site_rows, site_cols, cell), F32),
            vmem((site_rows + MARGIN, site_cols, band), F32),
            vmem((site_rows + MARGIN, site_cols + 8, band // 2), F32),
            vmem((site_rows + SPAN, site_cols + 8, cell), F32),
            vmem((site_rows + SPAN, site_cols + 8, cell), F32),
            vmem((rows * site_rows + MARGIN, site_cols, band), BF16),
            vmem((phases, MARGIN * site_cols + 16, cell), BF16),
            vmem((phases, MARGIN * site_cols + 16, cell), BF16),
            vmem((phases, (site_rows + SPAN) * 4, cell), BF16),
            vmem((phases, (site_rows + SPAN) * 4, cell), BF16),
            vmem((phases, MARGIN * site_cols + 16, cell), BF16),
            vmem((phases, MARGIN * site_cols + 16, cell), BF16),
            vmem((phases, (site_rows + SPAN) * 4, cell), BF16),
            vmem((phases, (site_rows + SPAN) * 4, cell), BF16),
            vmem((phases, 4, 16, cell), BF16),
            vmem((site_rows * 3 // 2, site_cols, 128), BF16),
            vmem((site_rows * 6, 128), BF16),
            vmem((atoms, sites), BF16),
            vmem((atoms // rows, rows * sites), BF16),
            vmem((rows, site_rows * 3 // 2, site_cols, 128), BF16),
            vmem((rows, site_rows * 6, 128), BF16),
            vmem((2, cols // 2, 2, 2 * owned, band), BF16),
            vmem((2, cols // 2, 2 * owned, band), BF16),
            vmem((2, cols // 2, 2 * owned, band), BF16),
            vmem((2, cols // 2, 2 * owned, band), BF16),
            dma((SPAN + 2,)),
            dma((phases, 8)), dma((phases, 8)),
            dma((rows,)), dma((rows,)),
            dma((rows,)), dma((rows,)),
            dma((rows,)), dma((rows,)),
            dma((2,)), dma((2,)),
            dma((2, cols // 2)), dma((2, cols // 2)),
        ],
        compiler_params=pltpu.CompilerParams(
            collective_id=0, has_side_effects=True, vmem_limit_bytes=int(53 * 2**20)
        ),
    )(picture, membrane.reshape(sites, atoms), dictionary)
    codes, new_dictionary, new_momentum = pl.pallas_call(
        finish,
        out_shape=tuple(jax.ShapeDtypeStruct(x.shape, x.dtype) for x in results),
        in_specs=[in_vmem] * 4,
        out_specs=(anywhere, in_vmem, in_vmem),
        scratch_shapes=[dma(())],
        compiler_params=pltpu.CompilerParams(vmem_limit_bytes=4 * 2**20),
    )(*results, momentum)
    return codes.reshape(membrane.shape), new_dictionary, new_momentum


def solution(mesh):
    return jax.shard_map(
        shards,
        mesh=mesh,
        in_specs=(P(None, "row", "col"), P("row", "col", None), P(), P(("row", "col"), None)),
        out_specs=(P("row", "col", None), P(("row", "col"), None), P(("row", "col"), None)),
        check_vma=False,
    )
```

```python
import functools

import jax
import jax.numpy as jnp
from jax import lax
from jax.experimental import pallas as pl
from jax.experimental.pallas import tpu as pltpu
from jax.sharding import PartitionSpec as P

STRIDE = 8
SPAN = 4
MARGIN = SPAN - 1
SWEEPS = 2

THRESHOLD = 0.25
RELAXATION = 0.1
DECAY = 0.9
LEARNING = 0.25
EPSILON = 1e-05

F32 = jnp.float32
BF16 = jnp.bfloat16
MESH = pl.DeviceIdType.MESH


def shrink(potential):
    return potential - jnp.clip(potential, -THRESHOLD, THRESHOLD)


def cells_of(picture):
    channels = picture.shape[0]
    x = picture.reshape(-1, STRIDE, 128)
    y_at = lax.broadcasted_iota(jnp.int32, (1, STRIDE, 128), 1)
    lane = lax.broadcasted_iota(jnp.int32, (1, STRIDE, 128), 2)
    for bit in (1, 2, 4):
        from_later = pltpu.roll(pltpu.roll(x, STRIDE - bit, 1), STRIDE * bit, 2)
        from_earlier = pltpu.roll(pltpu.roll(x, bit, 1), 128 - STRIDE * bit, 2)
        y_bit = (y_at & bit) != 0
        g_bit = (lane & (STRIDE * bit)) != 0
        x = jnp.where(y_bit == g_bit, x, jnp.where(g_bit, from_later, from_earlier))
    x = x.reshape(channels, -1, STRIDE, 128)
    turned = pltpu.roll(x.reshape(-1, STRIDE, 128), 64, 2).reshape(x.shape)
    lower = lane < 64
    left = jnp.concatenate(
        [jnp.where(lower, x[0], turned[1]), jnp.where(lower, turned[0], x[1])], axis=1
    )
    right = jnp.concatenate([x[2], turned[2]], axis=1)
    return jnp.concatenate([left, right[:, :, :64]], axis=2)


def tightened(x):
    n = x.shape[0] // 2
    ends = jnp.concatenate([x[:n, :, 128:], x[n:, :, 128:]], axis=2)
    return jnp.concatenate([x[:, :, :128], ends], axis=0)


def untightened(t):
    n = t.shape[0] * 2 // 3
    ends = jnp.concatenate([t[n:, :, :64], t[n:, :, 64:]], axis=0)
    return jnp.concatenate([t[:n], ends], axis=2)


def peers_of(rows, cols):
    offsets = {(j, 0) for j in range(rows)} | {(0, j) for j in range(0, cols, 2)}
    offsets |= {(j, k % cols) for j in range(rows) for k in (1, -1)}
    return sorted(offsets - {(0, 0)})


def kernel(
    rows, cols,
    picture_hbm, membrane_hbm, dictionary_hbm,
    codes_out, learning_out, atoms_out,
    picture_ref, dic, dic_t, pot, coding, cells_ref, acc, zbuf, cbuf, ext, wide,
    down_out, up_out, t_out, l_out, above_in, below_in, left_in, right_in, corner_in,
    res_ref, edge_ref,
    codes_t, strip_codes, strip_res, strip_edge, share_out, pair_in, summed, share_in,
    load_sem, spill_send, spill_recv,
    code_send, code_recv, res_send, res_recv, rim_send, rim_recv,
    pair_send, pair_recv, share_send, share_recv,
):
    site_rows, site_cols, cell = cells_ref.shape
    sites, atoms = pot.shape
    patch = dic.shape[1]
    band = patch // SPAN
    pair = band // 2
    scale = patch ** (-0.5)
    share = atoms // rows
    owned = learning_out.shape[0]
    me_r, me_c = lax.axis_index("row"), lax.axis_index("col")

    def at(dr, dc):
        return (lax.rem(me_r + dr % rows, rows), lax.rem(me_c + dc % cols, cols))

    def remote(src, dst, send, recv, dr, dc):
        return pltpu.make_async_remote_copy(
            src_ref=src, dst_ref=dst, send_sem=send, recv_sem=recv,
            device_id=at(dr, dc), device_id_type=MESH,
        )

    loads = [
        pltpu.make_async_copy(
            dictionary_hbm.at[:, pl.ds(d * band, band)],
            dic.at[:, pl.ds(d * band, band)],
            load_sem.at[d],
        )
        for d in range(SPAN)
    ]
    membrane_load = pltpu.make_async_copy(membrane_hbm, pot, load_sem.at[SPAN])
    picture_load = pltpu.make_async_copy(picture_hbm, picture_ref, load_sem.at[SPAN + 1])
    for load in [membrane_load] + loads[:1] + [picture_load] + loads[1:]:
        load.start()

    barrier = pltpu.get_barrier_semaphore()
    peers = peers_of(rows, cols)
    for dr, dc in peers:
        pl.semaphore_signal(barrier, inc=1, device_id=at(dr, dc), device_id_type=MESH)

    wide[rows * site_rows :] = jnp.zeros((MARGIN, site_cols, band), BF16)
    zbuf[...] = jnp.zeros_like(zbuf)
    cbuf[...] = jnp.zeros_like(cbuf)
    membrane_load.wait()
    coding[...] = shrink(pot[...]).astype(BF16)
    sent = []

    def send(copies):
        for copy in copies:
            copy.start()
        sent.extend(copies)

    def settle(keep=0):
        while len(sent) > keep:
            sent.pop(0).wait_send()

    sub = lax.broadcasted_iota(jnp.int32, (1, 8, cell), 1)
    low = sub < 4

    def packed(tall):
        n = tall.shape[0] // 2
        split = tall.reshape(n, 2, 8, cell)
        return split[:, 0] + pltpu.roll(split[:, 1], 4, 1)

    def unpacked(tight):
        n = tight.shape[0]
        both = jnp.stack([tight, pltpu.roll(tight, 4, 1)], axis=1)
        return jnp.where(low, both.reshape(2 * n, 8, cell), 0.0)

    def reconstruct(phase, meanwhile):
        for d in range(SPAN):
            if phase == 0:
                loads[d].wait()
            placed = jnp.dot(
                coding[...], dic[:, d * band : (d + 1) * band], preferred_element_type=F32
            ).reshape(site_rows, site_cols, band)
            if d == 0:
                acc[0:site_rows] = placed
            else:
                acc[d : d + site_rows - 1] += placed[: site_rows - 1]
                acc[d + site_rows - 1] = placed[site_rows - 1]
        zbuf[:, 0:site_cols] = acc[:, :, :pair]
        zbuf[:, site_cols:] = jnp.zeros((site_rows + MARGIN, 8, pair), F32)
        zbuf[:, 2 : site_cols + 2] += acc[:, :, pair:]
        every = zbuf[...]
        cbuf[: site_rows + MARGIN] = every[:, :, :cell]
        cbuf[: site_rows + MARGIN, 1 : site_cols + 3] += every[:, : site_cols + 2, cell:]
        ext[...] = cbuf[...] * -scale
        if phase == 0:
            picture_load.wait()
            cells_ref[...] = cells_of(picture_ref[...])
        ext[:site_rows, :site_cols] += cells_ref[...]
        beyond = packed(ext[:, site_cols:])
        within = packed(jnp.where(low, ext[:, :8], 0.0))
        tight = lambda part: part.reshape(-1, cell)
        tail, head = slice(site_rows // 2, None), slice(0, 2)
        last = phase == SWEEPS
        own_t = site_rows * 4
        main = MARGIN * site_cols
        corner = pl.ds(own_t, 16)

        def hop(k, src, dst, dr, dc):
            return remote(src, dst, spill_send.at[phase, k], spill_recv.at[phase, k], dr, dc)

        copies = []

        def go(*some):
            send(some)
            copies.extend(some)

        if phase == 0:
            pl.semaphore_wait(barrier, len(peers))
        t_out[phase] = tight(beyond).astype(BF16)
        reach = own_t if last else own_t + 16
        go(
            hop(0, t_out.at[phase, corner], corner_in.at[phase, 0], 1, 1),
            hop(2, t_out.at[phase, pl.ds(0, reach)], left_in.at[phase, pl.ds(0, reach)], 0, 1),
        )
        down_out[phase] = jnp.concatenate(
            [tight(ext[site_rows : site_rows + MARGIN, :site_cols]), tight(beyond[tail])]
        ).astype(BF16)
        reach = main if last else main + 16
        go(hop(1, down_out.at[phase, pl.ds(0, reach)], above_in.at[phase, pl.ds(0, reach)], 1, 0))
        if not last:
            l_out[phase] = tight(within).astype(BF16)
            go(
                hop(3, l_out.at[phase, pl.ds(0, 16)], corner_in.at[phase, 1], -1, -1),
                hop(4, l_out.at[phase, corner], corner_in.at[phase, 2], 1, -1),
                hop(5, t_out.at[phase, pl.ds(0, 16)], corner_in.at[phase, 3], -1, 1),
                hop(7, l_out.at[phase], right_in.at[phase], 0, -1),
            )
            up_out[phase] = jnp.concatenate(
                [tight(ext[:MARGIN, :site_cols]), tight(beyond[head])]
            ).astype(BF16)
            go(hop(6, up_out.at[phase], below_in.at[phase], -1, 0))
        meanwhile()
        settle(len(copies) + (rows - 1 if last else 0))
        return copies

    has_above, has_below = me_r > 0, me_r < rows - 1
    has_left, has_right = me_c > 0, me_c < cols - 1

    def loose(ref_part):
        return unpacked(ref_part.astype(F32).reshape(-1, 8, cell))

    def gather_spill(phase, copies):
        last = phase == SWEEPS
        for copy in copies:
            copy.wait_recv()
        main = MARGIN * site_cols
        own_t = site_rows * 4
        own, far_r, far_c = slice(0, site_rows), slice(site_rows, None), slice(site_cols, None)
        ext[:MARGIN, :site_cols] += jnp.where(
            has_above, above_in[phase, :main].astype(F32).reshape(MARGIN, site_cols, cell), 0.0
        )
        reach = own_t if last else own_t + 16
        ext[: reach // 4, :8] += jnp.where(has_left, loose(left_in[phase, :reach]), 0.0)
        ext[:SPAN, :8] += jnp.where(
            jnp.logical_and(has_above, has_left), loose(corner_in[phase, 0]), 0.0
        )
        if last:
            return
        ext[far_r, :8] += jnp.where(has_left, loose(corner_in[phase, 3]), 0.0)
        side = ext[:, far_c] + loose(right_in[phase])
        side_head = side[:SPAN] + jnp.where(
            has_above, loose(above_in[phase, main:]) + loose(corner_in[phase, 2]), 0.0
        )
        side_tail = side[site_rows:] + loose(below_in[phase, main:]) + loose(corner_in[phase, 1])
        ext[:, far_c] = jnp.where(has_right, side, 0.0)
        ext[:SPAN, far_c] = jnp.where(has_right, side_head, 0.0)
        ext[far_r, far_c] = jnp.where(jnp.logical_and(has_right, has_below), side_tail, 0.0)
        under = ext[site_rows : site_rows + MARGIN, :site_cols] + below_in[phase, :main].astype(
            F32
        ).reshape(MARGIN, site_cols, cell)
        ext[site_rows : site_rows + MARGIN, :site_cols] = jnp.where(has_below, under, 0.0)

    def widen(n):
        x = ext[:n]
        return jnp.concatenate(
            [x[:, k : k + site_cols] for k in range(SPAN)], axis=2
        ).astype(BF16)

    def turn_dictionary():
        for first in range(0, atoms, 256):
            for d in range(SPAN):
                dic_t[d * band : (d + 1) * band, first : first + 256] = dic[
                    first : first + 256, d * band : (d + 1) * band
                ].T

    for sweep in range(SWEEPS):
        meanwhile = turn_dictionary if sweep == 0 else lambda: None
        gather_spill(sweep, reconstruct(sweep, meanwhile))
        wide[: site_rows + MARGIN] = widen(site_rows + MARGIN)
        last = sweep == SWEEPS - 1
        step = 256 if atoms % 256 == 0 else 128
        for first in range(0, atoms, step):
            drive = jnp.zeros((sites, step), F32)
            for d in range(SPAN):
                drive += jnp.dot(
                    wide[d : d + site_rows].reshape(sites, band),
                    dic_t[d * band : (d + 1) * band, first : first + step],
                    preferred_element_type=F32,
                )
            old = pot[:, first : first + step]
            new = old + RELAXATION * (drive * scale + shrink(old) - old)
            codes = shrink(new)
            coding[:, first : first + step] = codes.astype(BF16)
            if last:
                codes_out[:, first : first + step] = codes
            else:
                pot[:, first : first + step] = new

    def share_of(row):
        return codes_t.at[pl.ds(pl.multiple_of(row * share, share), share)]

    def place_of(row):
        return strip_codes.at[:, pl.ds(pl.multiple_of(row * sites, sites), sites)]

    code_copies = [
        remote(share_of(at(j, 0)[0]), place_of(me_r), code_send.at[j], code_recv.at[j], j, 0)
        for j in range(1, rows)
    ]

    def give_codes():
        codes_t[...] = codes_out[...].T.astype(BF16)
        send(code_copies)
        place_of(me_r)[...] = share_of(me_r)[...]

    gather_spill(SWEEPS, reconstruct(SWEEPS, give_codes))
    residual = ext[:site_rows, :site_cols].astype(BF16).astype(F32)
    res_ref[...] = tightened(residual).astype(BF16)
    left_cols = packed(jnp.where(low, residual[:, :8], 0.0))
    edge_ref[...] = tightened(left_cols).reshape(-1, 128).astype(BF16)
    rim_copies = [
        remote(edge_ref, strip_edge.at[j], rim_send.at[j], rim_recv.at[j], j, -1)
        for j in range(rows)
    ]
    res_copies = [None] + [
        remote(res_ref, strip_res.at[j], res_send.at[j], res_recv.at[j], j, 0)
        for j in range(1, rows)
    ]
    for j in range(rows):
        send([rim_copies[j]] + ([res_copies[j]] if j else []))
    settle(2 * rows - 1)
    for j in range(rows):
        rim_copies[j].wait_recv()
        if j:
            res_copies[j].wait_recv()
        block = strip_res[j] if j else res_ref[...]
        ext[:site_rows, :site_cols] = untightened(block.astype(F32))
        ext[:site_rows, site_cols:] = jnp.where(has_right, unpacked(untightened(strip_edge[j].astype(F32).reshape(-1, 8, 128))), 0.0)
        source = at(-j, 0)[0]
        wide[pl.ds(source * site_rows, site_rows)] = widen(site_rows)
    for copy in code_copies:
        copy.wait_recv()

    tall = rows * site_rows
    core = lax.rem(me_c, 2)
    chip = lax.div(me_c, 2)
    chips = cols // 2
    twin = (me_r, me_c + 1 - 2 * core)
    pair_copies, share_copies = [], []
    for e in range(2):
        parts = [
            jnp.dot(
                strip_codes[...],
                wide[d : d + tall].reshape(tall * site_cols, band),
                preferred_element_type=F32,
            ).reshape(chips, 2, owned, band)
            for d in (e, e + 2)
        ]
        share_out[e] = jnp.concatenate(parts, axis=2).astype(BF16)
        pair_copies.append(
            pltpu.make_async_remote_copy(
                src_ref=share_out.at[e, :, 1 - core], dst_ref=pair_in.at[e],
                send_sem=pair_send.at[e], recv_sem=pair_recv.at[e],
                device_id=twin, device_id_type=MESH,
            )
        )
        send(pair_copies[e:])
    for e in range(2):
        pair_copies[e].wait_recv()
        summed[e] = (share_out[e, :, core].astype(F32) + pair_in[e].astype(F32)).astype(BF16)
    share_copies = [
        remote(summed.at[:, lax.rem(chip + j, chips)], share_in.at[:, j],
               share_send.at[0, j], share_recv.at[0, j], 0, 2 * j)
        for j in range(1, chips)
    ]
    send(share_copies)
    settle(chips - 1)
    for copy in share_copies:
        copy.wait_recv()
    for e in range(2):
        total = summed[e, chip].astype(F32)
        for j in range(1, chips):
            total += share_in[e, j].astype(F32)
        for k in range(2):
            span = pl.ds((e + 2 * k) * band, band)
            learning_out[:, span] = total[k * owned : (k + 1) * owned] * scale
    tile = 2 * owned
    index = me_r * cols + me_c
    first = pl.multiple_of(lax.div(index, 2) * tile, tile)
    both = dic[pl.ds(first, tile)].astype(F32)
    atoms_out[...] = jnp.where(lax.rem(index, 2) == 1, both[owned:], both[:owned])
    settle()


def finish(
    codes_ref, learning_ref, atoms_ref, momentum_ref,
    codes_out, dictionary_out, momentum_out, sem,
):
    codes_copy = pltpu.make_async_copy(codes_ref, codes_out, sem)
    codes_copy.start()
    momentum = DECAY * momentum_ref[...] + learning_ref[...]
    weights = atoms_ref[...] + LEARNING * momentum
    momentum_out[...] = momentum
    dictionary_out[...] = weights * lax.rsqrt(
        jnp.mean(weights * weights, axis=1, keepdims=True) + EPSILON
    )
    codes_copy.wait()


def shards(picture, membrane, dictionary, momentum):
    site_rows, site_cols, atoms = membrane.shape
    sites = site_rows * site_cols
    patch = dictionary.shape[1]
    cell = patch // SPAN // SPAN
    band = patch // SPAN
    owned = momentum.shape[0]
    rows, cols = lax.axis_size("row"), lax.axis_size("col")
    phases = SWEEPS + 1
    vmem, dma = pltpu.VMEM, pltpu.SemaphoreType.DMA
    anywhere = pl.BlockSpec(memory_space=pltpu.HBM)
    in_vmem = pl.BlockSpec(memory_space=pltpu.VMEM)
    results = pl.pallas_call(
        functools.partial(kernel, rows, cols),
        out_shape=(
            jax.ShapeDtypeStruct((sites, atoms), F32),
            jax.ShapeDtypeStruct((owned, patch), F32),
            jax.ShapeDtypeStruct((owned, patch), F32),
        ),
        in_specs=[anywhere, anywhere, anywhere],
        out_specs=(in_vmem, in_vmem, in_vmem),
        scratch_shapes=[
            vmem(picture.shape, F32),
            vmem((atoms, patch), BF16),
            vmem((patch, atoms), BF16),
            vmem((sites, atoms), F32),
            vmem((sites, atoms), BF16),
            vmem((site_rows, site_cols, cell), F32),
            vmem((site_rows + MARGIN, site_cols, band), F32),
            vmem((site_rows + MARGIN, site_cols + 8, band // 2), F32),
            vmem((site_rows + SPAN, site_cols + 8, cell), F32),
            vmem((site_rows + SPAN, site_cols + 8, cell), F32),
            vmem((rows * site_rows + MARGIN, site_cols, band), BF16),
            vmem((phases, MARGIN * site_cols + 16, cell), BF16),
            vmem((phases, MARGIN * site_cols + 16, cell), BF16),
            vmem((phases, (site_rows + SPAN) * 4, cell), BF16),
            vmem((phases, (site_rows + SPAN) * 4, cell), BF16),
            vmem((phases, MARGIN * site_cols + 16, cell), BF16),
            vmem((phases, MARGIN * site_cols + 16, cell), BF16),
            vmem((phases, (site_rows + SPAN) * 4, cell), BF16),
            vmem((phases, (site_rows + SPAN) * 4, cell), BF16),
            vmem((phases, 4, 16, cell), BF16),
            vmem((site_rows * 3 // 2, site_cols, 128), BF16),
            vmem((site_rows * 6, 128), BF16),
            vmem((atoms, sites), BF16),
            vmem((atoms // rows, rows * sites), BF16),
            vmem((rows, site_rows * 3 // 2, site_cols, 128), BF16),
            vmem((rows, site_rows * 6, 128), BF16),
            vmem((2, cols // 2, 2, 2 * owned, band), BF16),
            vmem((2, cols // 2, 2 * owned, band), BF16),
            vmem((2, cols // 2, 2 * owned, band), BF16),
            vmem((2, cols // 2, 2 * owned, band), BF16),
            dma((SPAN + 2,)),
            dma((phases, 8)), dma((phases, 8)),
            dma((rows,)), dma((rows,)),
            dma((rows,)), dma((rows,)),
            dma((rows,)), dma((rows,)),
            dma((2,)), dma((2,)),
            dma((2, cols // 2)), dma((2, cols // 2)),
        ],
        compiler_params=pltpu.CompilerParams(
            collective_id=0, has_side_effects=True, vmem_limit_bytes=int(53 * 2**20)
        ),
    )(picture, membrane.reshape(sites, atoms), dictionary)
    codes, new_dictionary, new_momentum = pl.pallas_call(
        finish,
        out_shape=tuple(jax.ShapeDtypeStruct(x.shape, x.dtype) for x in results),
        in_specs=[in_vmem] * 4,
        out_specs=(anywhere, in_vmem, in_vmem),
        scratch_shapes=[dma(())],
        compiler_params=pltpu.CompilerParams(vmem_limit_bytes=4 * 2**20),
    )(*results, momentum)
    return codes.reshape(membrane.shape), new_dictionary, new_momentum


def solution(mesh):
    return jax.shard_map(
        shards,
        mesh=mesh,
        in_specs=(P(None, "row", "col"), P("row", "col", None), P(), P(("row", "col"), None)),
        out_specs=(P("row", "col", None), P(("row", "col"), None), P(("row", "col"), None)),
        check_vma=False,
    )
```

```python
import functools

import jax
import jax.numpy as jnp
from jax import lax
from jax.experimental import pallas as pl
from jax.experimental.pallas import tpu as pltpu
from jax.sharding import PartitionSpec as P

STRIDE = 8
SPAN = 4
MARGIN = SPAN - 1
SWEEPS = 2

THRESHOLD = 0.25
RELAXATION = 0.1
DECAY = 0.9
LEARNING = 0.25
EPSILON = 1e-05

F32 = jnp.float32
BF16 = jnp.bfloat16
MESH = pl.DeviceIdType.MESH


def shrink(potential):
    return potential - jnp.clip(potential, -THRESHOLD, THRESHOLD)


def cells_of(picture):
    channels = picture.shape[0]
    x = picture.reshape(-1, STRIDE, 128)
    y_at = lax.broadcasted_iota(jnp.int32, (1, STRIDE, 128), 1)
    lane = lax.broadcasted_iota(jnp.int32, (1, STRIDE, 128), 2)
    for bit in (1, 2, 4):
        from_later = pltpu.roll(pltpu.roll(x, STRIDE - bit, 1), STRIDE * bit, 2)
        from_earlier = pltpu.roll(pltpu.roll(x, bit, 1), 128 - STRIDE * bit, 2)
        y_bit = (y_at & bit) != 0
        g_bit = (lane & (STRIDE * bit)) != 0
        x = jnp.where(y_bit == g_bit, x, jnp.where(g_bit, from_later, from_earlier))
    x = x.reshape(channels, -1, STRIDE, 128)
    turned = pltpu.roll(x.reshape(-1, STRIDE, 128), 64, 2).reshape(x.shape)
    lower = lane < 64
    left = jnp.concatenate(
        [jnp.where(lower, x[0], turned[1]), jnp.where(lower, turned[0], x[1])], axis=1
    )
    right = jnp.concatenate([x[2], turned[2]], axis=1)
    return jnp.concatenate([left, right[:, :, :64]], axis=2)


def tightened(x):
    n = x.shape[0] // 2
    ends = jnp.concatenate([x[:n, :, 128:], x[n:, :, 128:]], axis=2)
    return jnp.concatenate([x[:, :, :128], ends], axis=0)


def untightened(t):
    n = t.shape[0] * 2 // 3
    ends = jnp.concatenate([t[n:, :, :64], t[n:, :, 64:]], axis=0)
    return jnp.concatenate([t[:n], ends], axis=2)


def peers_of(rows, cols):
    offsets = {(j, 0) for j in range(rows)} | {(0, j) for j in range(0, cols, 2)}
    offsets |= {(j, k % cols) for j in range(rows) for k in (1, -1)}
    return sorted(offsets - {(0, 0)})


def kernel(
    rows, cols,
    picture_hbm, membrane_hbm, dictionary_hbm,
    codes_out, learning_out, atoms_out,
    picture_ref, dic, dic_t, pot, coding, cells_ref, acc, zbuf, cbuf, ext, wide,
    down_out, up_out, t_out, l_out, above_in, below_in, left_in, right_in, corner_in,
    res_ref, edge_ref,
    codes_t, strip_codes, strip_res, strip_edge, share_out, pair_in, summed, share_in,
    load_sem, spill_send, spill_recv,
    code_send, code_recv, res_send, res_recv, rim_send, rim_recv,
    pair_send, pair_recv, share_send, share_recv,
):
    site_rows, site_cols, cell = cells_ref.shape
    sites, atoms = pot.shape
    patch = dic.shape[1]
    band = patch // SPAN
    pair = band // 2
    scale = patch ** (-0.5)
    share = atoms // rows
    owned = learning_out.shape[0]
    me_r, me_c = lax.axis_index("row"), lax.axis_index("col")

    def at(dr, dc):
        return (lax.rem(me_r + dr % rows, rows), lax.rem(me_c + dc % cols, cols))

    def remote(src, dst, send, recv, dr, dc):
        return pltpu.make_async_remote_copy(
            src_ref=src, dst_ref=dst, send_sem=send, recv_sem=recv,
            device_id=at(dr, dc), device_id_type=MESH,
        )

    loads = [
        pltpu.make_async_copy(
            dictionary_hbm.at[:, pl.ds(d * band, band)],
            dic.at[:, pl.ds(d * band, band)],
            load_sem.at[d],
        )
        for d in range(SPAN)
    ]
    membrane_load = pltpu.make_async_copy(membrane_hbm, pot, load_sem.at[SPAN])
    picture_load = pltpu.make_async_copy(picture_hbm, picture_ref, load_sem.at[SPAN + 1])
    for load in [membrane_load] + loads[:1] + [picture_load] + loads[1:]:
        load.start()

    barrier = pltpu.get_barrier_semaphore()
    peers = peers_of(rows, cols)
    for dr, dc in peers:
        pl.semaphore_signal(barrier, inc=1, device_id=at(dr, dc), device_id_type=MESH)

    wide[rows * site_rows :] = jnp.zeros((MARGIN, site_cols, band), BF16)
    zbuf[...] = jnp.zeros_like(zbuf)
    cbuf[...] = jnp.zeros_like(cbuf)
    membrane_load.wait()
    coding[...] = shrink(pot[...]).astype(BF16)
    sent = []

    def send(copies):
        for copy in copies:
            copy.start()
        sent.extend(copies)

    def settle(keep=0):
        while len(sent) > keep:
            sent.pop(0).wait_send()

    sub = lax.broadcasted_iota(jnp.int32, (1, 8, cell), 1)
    low = sub < 4

    def packed(tall):
        n = tall.shape[0] // 2
        split = tall.reshape(n, 2, 8, cell)
        return split[:, 0] + pltpu.roll(split[:, 1], 4, 1)

    def unpacked(tight):
        n = tight.shape[0]
        both = jnp.stack([tight, pltpu.roll(tight, 4, 1)], axis=1)
        return jnp.where(low, both.reshape(2 * n, 8, cell), 0.0)

    def reconstruct(phase, meanwhile):
        for d in range(SPAN):
            if phase == 0:
                loads[d].wait()
            placed = jnp.dot(
                coding[...], dic[:, d * band : (d + 1) * band], preferred_element_type=F32
            ).reshape(site_rows, site_cols, band)
            if d == 0:
                acc[0:site_rows] = placed
            else:
                acc[d : d + site_rows - 1] += placed[: site_rows - 1]
                acc[d + site_rows - 1] = placed[site_rows - 1]
        zbuf[:, 0:site_cols] = acc[:, :, :pair]
        zbuf[:, site_cols:] = jnp.zeros((site_rows + MARGIN, 8, pair), F32)
        zbuf[:, 2 : site_cols + 2] += acc[:, :, pair:]
        every = zbuf[...]
        cbuf[: site_rows + MARGIN] = every[:, :, :cell]
        cbuf[: site_rows + MARGIN, 1 : site_cols + 3] += every[:, : site_cols + 2, cell:]
        ext[...] = cbuf[...] * -scale
        if phase == 0:
            picture_load.wait()
            cells_ref[...] = cells_of(picture_ref[...])
        ext[:site_rows, :site_cols] += cells_ref[...]
        beyond = packed(ext[:, site_cols:])
        within = packed(jnp.where(low, ext[:, :8], 0.0))
        tight = lambda part: part.reshape(-1, cell)
        tail, head = slice(site_rows // 2, None), slice(0, 2)
        last = phase == SWEEPS
        t_out[phase] = tight(beyond).astype(BF16)
        down_out[phase] = jnp.concatenate(
            [tight(ext[site_rows : site_rows + MARGIN, :site_cols]), tight(beyond[tail])]
        ).astype(BF16)
        if not last:
            l_out[phase] = tight(within).astype(BF16)
            up_out[phase] = jnp.concatenate(
                [tight(ext[:MARGIN, :site_cols]), tight(beyond[head])]
            ).astype(BF16)
        own_t = site_rows * 4
        main = MARGIN * site_cols
        corner = pl.ds(own_t, 16)

        def hop(k, src, dst, dr, dc):
            return remote(src, dst, spill_send.at[phase, k], spill_recv.at[phase, k], dr, dc)

        if last:
            copies = [
                hop(0, t_out.at[phase, corner], corner_in.at[phase, 0], 1, 1),
                hop(1, down_out.at[phase, pl.ds(0, main)], above_in.at[phase, pl.ds(0, main)], 1, 0),
                hop(2, t_out.at[phase, pl.ds(0, own_t)], left_in.at[phase, pl.ds(0, own_t)], 0, 1),
            ]
        else:
            copies = [
                hop(0, t_out.at[phase, corner], corner_in.at[phase, 0], 1, 1),
                hop(3, l_out.at[phase, pl.ds(0, 16)], corner_in.at[phase, 1], -1, -1),
                hop(4, l_out.at[phase, corner], corner_in.at[phase, 2], 1, -1),
                hop(5, t_out.at[phase, pl.ds(0, 16)], corner_in.at[phase, 3], -1, 1),
                hop(1, down_out.at[phase], above_in.at[phase], 1, 0),
                hop(6, up_out.at[phase], below_in.at[phase], -1, 0),
                hop(2, t_out.at[phase], left_in.at[phase], 0, 1),
                hop(7, l_out.at[phase], right_in.at[phase], 0, -1),
            ]
        if phase == 0:
            pl.semaphore_wait(barrier, len(peers))
        send(copies)
        meanwhile()
        settle(len(copies) + (rows - 1 if last else 0))
        return copies

    has_above, has_below = me_r > 0, me_r < rows - 1
    has_left, has_right = me_c > 0, me_c < cols - 1

    def loose(ref_part):
        return unpacked(ref_part.astype(F32).reshape(-1, 8, cell))

    def gather_spill(phase, copies):
        last = phase == SWEEPS
        for copy in copies:
            copy.wait_recv()
        main = MARGIN * site_cols
        own_t = site_rows * 4
        own, far_r, far_c = slice(0, site_rows), slice(site_rows, None), slice(site_cols, None)
        ext[:MARGIN, :site_cols] += jnp.where(
            has_above, above_in[phase, :main].astype(F32).reshape(MARGIN, site_cols, cell), 0.0
        )
        reach = own_t if last else own_t + 16
        ext[: reach // 4, :8] += jnp.where(has_left, loose(left_in[phase, :reach]), 0.0)
        ext[:SPAN, :8] += jnp.where(
            jnp.logical_and(has_above, has_left), loose(corner_in[phase, 0]), 0.0
        )
        if last:
            return
        ext[far_r, :8] += jnp.where(has_left, loose(corner_in[phase, 3]), 0.0)
        side = ext[:, far_c] + loose(right_in[phase])
        side_head = side[:SPAN] + jnp.where(
            has_above, loose(above_in[phase, main:]) + loose(corner_in[phase, 2]), 0.0
        )
        side_tail = side[site_rows:] + loose(below_in[phase, main:]) + loose(corner_in[phase, 1])
        ext[:, far_c] = jnp.where(has_right, side, 0.0)
        ext[:SPAN, far_c] = jnp.where(has_right, side_head, 0.0)
        ext[far_r, far_c] = jnp.where(jnp.logical_and(has_right, has_below), side_tail, 0.0)
        under = ext[site_rows : site_rows + MARGIN, :site_cols] + below_in[phase, :main].astype(
            F32
        ).reshape(MARGIN, site_cols, cell)
        ext[site_rows : site_rows + MARGIN, :site_cols] = jnp.where(has_below, under, 0.0)

    def widen(n):
        x = ext[:n]
        return jnp.concatenate(
            [x[:, k : k + site_cols] for k in range(SPAN)], axis=2
        ).astype(BF16)

    def turn_dictionary():
        for first in range(0, atoms, 256):
            for d in range(SPAN):
                dic_t[d * band : (d + 1) * band, first : first + 256] = dic[
                    first : first + 256, d * band : (d + 1) * band
                ].T

    for sweep in range(SWEEPS):
        meanwhile = turn_dictionary if sweep == 0 else lambda: None
        gather_spill(sweep, reconstruct(sweep, meanwhile))
        wide[: site_rows + MARGIN] = widen(site_rows + MARGIN)
        last = sweep == SWEEPS - 1
        step = 256 if atoms % 256 == 0 else 128
        for first in range(0, atoms, step):
            drive = jnp.zeros((sites, step), F32)
            for d in range(SPAN):
                drive += jnp.dot(
                    wide[d : d + site_rows].reshape(sites, band),
                    dic_t[d * band : (d + 1) * band, first : first + step],
                    preferred_element_type=F32,
                )
            old = pot[:, first : first + step]
            new = old + RELAXATION * (drive * scale + shrink(old) - old)
            codes = shrink(new)
            coding[:, first : first + step] = codes.astype(BF16)
            if last:
                codes_out[:, first : first + step] = codes
            else:
                pot[:, first : first + step] = new

    def share_of(row):
        return codes_t.at[pl.ds(pl.multiple_of(row * share, share), share)]

    def place_of(row):
        return strip_codes.at[:, pl.ds(pl.multiple_of(row * sites, sites), sites)]

    code_copies = [
        remote(share_of(at(j, 0)[0]), place_of(me_r), code_send.at[j], code_recv.at[j], j, 0)
        for j in range(1, rows)
    ]

    def give_codes():
        codes_t[...] = codes_out[...].T.astype(BF16)
        send(code_copies)
        place_of(me_r)[...] = share_of(me_r)[...]

    gather_spill(SWEEPS, reconstruct(SWEEPS, give_codes))
    residual = ext[:site_rows, :site_cols].astype(BF16).astype(F32)
    res_ref[...] = tightened(residual).astype(BF16)
    left_cols = packed(jnp.where(low, residual[:, :8], 0.0))
    edge_ref[...] = tightened(left_cols).reshape(-1, 128).astype(BF16)
    rim_copies = [
        remote(edge_ref, strip_edge.at[j], rim_send.at[j], rim_recv.at[j], j, -1)
        for j in range(rows)
    ]
    res_copies = [None] + [
        remote(res_ref, strip_res.at[j], res_send.at[j], res_recv.at[j], j, 0)
        for j in range(1, rows)
    ]
    for j in range(rows):
        send([rim_copies[j]] + ([res_copies[j]] if j else []))
    settle(2 * rows - 1)
    for j in range(rows):
        rim_copies[j].wait_recv()
        if j:
            res_copies[j].wait_recv()
        block = strip_res[j] if j else res_ref[...]
        ext[:site_rows, :site_cols] = untightened(block.astype(F32))
        ext[:site_rows, site_cols:] = jnp.where(has_right, unpacked(untightened(strip_edge[j].astype(F32).reshape(-1, 8, 128))), 0.0)
        source = at(-j, 0)[0]
        wide[pl.ds(source * site_rows, site_rows)] = widen(site_rows)
    for copy in code_copies:
        copy.wait_recv()

    tall = rows * site_rows
    core = lax.rem(me_c, 2)
    chip = lax.div(me_c, 2)
    chips = cols // 2
    twin = (me_r, me_c + 1 - 2 * core)
    pair_copies, share_copies = [], []
    for e in range(2):
        parts = [
            jnp.dot(
                strip_codes[...],
                wide[d : d + tall].reshape(tall * site_cols, band),
                preferred_element_type=F32,
            ).reshape(chips, 2, owned, band)
            for d in (e, e + 2)
        ]
        share_out[e] = jnp.concatenate(parts, axis=2).astype(BF16)
        pair_copies.append(
            pltpu.make_async_remote_copy(
                src_ref=share_out.at[:, :, 1 - core], dst_ref=pair_in,
                send_sem=pair_send.at[e], recv_sem=pair_recv.at[e],
                device_id=twin, device_id_type=MESH,
            )
        )
        if e == 1:
            send(pair_copies[1:])
    for e in range(2):
        if e == 0:
            pair_copies[1].wait_recv()
        summed[e] = (share_out[e, :, core].astype(F32) + pair_in[e].astype(F32)).astype(BF16)
    share_copies = [
        remote(summed.at[:, lax.rem(chip + j, chips)], share_in.at[:, j],
               share_send.at[0, j], share_recv.at[0, j], 0, 2 * j)
        for j in range(1, chips)
    ]
    send(share_copies)
    settle(chips - 1)
    for copy in share_copies:
        copy.wait_recv()
    for e in range(2):
        total = summed[e, chip].astype(F32)
        for j in range(1, chips):
            total += share_in[e, j].astype(F32)
        for k in range(2):
            span = pl.ds((e + 2 * k) * band, band)
            learning_out[:, span] = total[k * owned : (k + 1) * owned] * scale
    tile = 2 * owned
    index = me_r * cols + me_c
    first = pl.multiple_of(lax.div(index, 2) * tile, tile)
    both = dic[pl.ds(first, tile)].astype(F32)
    atoms_out[...] = jnp.where(lax.rem(index, 2) == 1, both[owned:], both[:owned])
    settle()


def finish(
    codes_ref, learning_ref, atoms_ref, momentum_ref,
    codes_out, dictionary_out, momentum_out, sem,
):
    codes_copy = pltpu.make_async_copy(codes_ref, codes_out, sem)
    codes_copy.start()
    momentum = DECAY * momentum_ref[...] + learning_ref[...]
    weights = atoms_ref[...] + LEARNING * momentum
    momentum_out[...] = momentum
    dictionary_out[...] = weights * lax.rsqrt(
        jnp.mean(weights * weights, axis=1, keepdims=True) + EPSILON
    )
    codes_copy.wait()


def shards(picture, membrane, dictionary, momentum):
    site_rows, site_cols, atoms = membrane.shape
    sites = site_rows * site_cols
    patch = dictionary.shape[1]
    cell = patch // SPAN // SPAN
    band = patch // SPAN
    owned = momentum.shape[0]
    rows, cols = lax.axis_size("row"), lax.axis_size("col")
    phases = SWEEPS + 1
    vmem, dma = pltpu.VMEM, pltpu.SemaphoreType.DMA
    anywhere = pl.BlockSpec(memory_space=pltpu.HBM)
    in_vmem = pl.BlockSpec(memory_space=pltpu.VMEM)
    results = pl.pallas_call(
        functools.partial(kernel, rows, cols),
        out_shape=(
            jax.ShapeDtypeStruct((sites, atoms), F32),
            jax.ShapeDtypeStruct((owned, patch), F32),
            jax.ShapeDtypeStruct((owned, patch), F32),
        ),
        in_specs=[anywhere, anywhere, anywhere],
        out_specs=(in_vmem, in_vmem, in_vmem),
        scratch_shapes=[
            vmem(picture.shape, F32),
            vmem((atoms, patch), BF16),
            vmem((patch, atoms), BF16),
            vmem((sites, atoms), F32),
            vmem((sites, atoms), BF16),
            vmem((site_rows, site_cols, cell), F32),
            vmem((site_rows + MARGIN, site_cols, band), F32),
            vmem((site_rows + MARGIN, site_cols + 8, band // 2), F32),
            vmem((site_rows + SPAN, site_cols + 8, cell), F32),
            vmem((site_rows + SPAN, site_cols + 8, cell), F32),
            vmem((rows * site_rows + MARGIN, site_cols, band), BF16),
            vmem((phases, MARGIN * site_cols + 16, cell), BF16),
            vmem((phases, MARGIN * site_cols + 16, cell), BF16),
            vmem((phases, (site_rows + SPAN) * 4, cell), BF16),
            vmem((phases, (site_rows + SPAN) * 4, cell), BF16),
            vmem((phases, MARGIN * site_cols + 16, cell), BF16),
            vmem((phases, MARGIN * site_cols + 16, cell), BF16),
            vmem((phases, (site_rows + SPAN) * 4, cell), BF16),
            vmem((phases, (site_rows + SPAN) * 4, cell), BF16),
            vmem((phases, 4, 16, cell), BF16),
            vmem((site_rows * 3 // 2, site_cols, 128), BF16),
            vmem((site_rows * 6, 128), BF16),
            vmem((atoms, sites), BF16),
            vmem((atoms // rows, rows * sites), BF16),
            vmem((rows, site_rows * 3 // 2, site_cols, 128), BF16),
            vmem((rows, site_rows * 6, 128), BF16),
            vmem((2, cols // 2, 2, 2 * owned, band), BF16),
            vmem((2, cols // 2, 2 * owned, band), BF16),
            vmem((2, cols // 2, 2 * owned, band), BF16),
            vmem((2, cols // 2, 2 * owned, band), BF16),
            dma((SPAN + 2,)),
            dma((phases, 8)), dma((phases, 8)),
            dma((rows,)), dma((rows,)),
            dma((rows,)), dma((rows,)),
            dma((rows,)), dma((rows,)),
            dma((2,)), dma((2,)),
            dma((2, cols // 2)), dma((2, cols // 2)),
        ],
        compiler_params=pltpu.CompilerParams(
            collective_id=0, has_side_effects=True, vmem_limit_bytes=int(53 * 2**20)
        ),
    )(picture, membrane.reshape(sites, atoms), dictionary)
    codes, new_dictionary, new_momentum = pl.pallas_call(
        finish,
        out_shape=tuple(jax.ShapeDtypeStruct(x.shape, x.dtype) for x in results),
        in_specs=[in_vmem] * 4,
        out_specs=(anywhere, in_vmem, in_vmem),
        scratch_shapes=[dma(())],
        compiler_params=pltpu.CompilerParams(vmem_limit_bytes=4 * 2**20),
    )(*results, momentum)
    return codes.reshape(membrane.shape), new_dictionary, new_momentum


def solution(mesh):
    return jax.shard_map(
        shards,
        mesh=mesh,
        in_specs=(P(None, "row", "col"), P("row", "col", None), P(), P(("row", "col"), None)),
        out_specs=(P("row", "col", None), P(("row", "col"), None), P(("row", "col"), None)),
        check_vma=False,
    )
```
